32 devices in a mesh: peer: 8 (over z, x), group: 4 (over y, core).
Axes of the slice: x: 2, y: 2, z: 4, core: 2. Of those that a mesh axis runs over, the one named last changes fastest.
Arguments:
- view_descriptors: bfloat16 [3072, 1536], P('peer'), may hold values from -6 to 6
- embedding_matrix: bfloat16 [1536, 1536], replicated, may hold values from -0.15625 to 0.15625
- picture_of_view: int32 [3072], P('peer'), may hold values from 0 to 6143
- filled_view_places: int32 [8], P('peer'), may hold values from 96 to 384, as said below
- companion_masks: int32 [4], P('group'), may hold values from 1 to 7, as said below
- score_scale: float32 [1], replicated, may hold values from 4 to 16
- score_shift: float32 [1], replicated, may hold values from -4 to -1
Outputs:
- projector_grad: float32 [12288, 1536], P('peer', 'group')
- block_loss: float32 [8, 4], P('peer', 'group')
The draws below stay inside these ranges and needn't reach their ends.
Inputs may be any that keep to these rules, and one draw needn't show every extreme that they name: `companion_masks`: entries are distinct partner masks from 1 to 6 in random order, and one of them is replaced by the largest mask 7. `filled_view_places`: some block is full.
All inputs are finite; a program needn't handle non-finite values.
Results may differ from the reference program's by a relative error of at most 0.0049.
Values may be sent and summed in bfloat16 or wider, within the bound.
No kernel may reach another device: no remote copies, remote signals or barrier semaphores. Data moves between devices by JAX's collectives and lax.ppermute only.
A program may use at most 64 MiB of HBM per device.

```python
import math
import jax
import jax.numpy as jnp
from jax import lax

D = 1536
ROWS = 384
ROUNDS_DEV = 1
CROPS = 3072
N_PEER = 8
N_GROUP = 4


def draw_filled_view_places(key, part):
    key = jax.random.fold_in(key, 11)
    values = jax.random.randint(jax.random.fold_in(key, 1), (N_PEER,), ROWS // 4, ROWS + 1)
    place = jax.random.randint(jax.random.fold_in(key, 2), (), 0, N_PEER)
    return values.at[place].set(ROWS).astype(jnp.int32)


def draw_companion_masks(key, part):
    key = jax.random.fold_in(key, 23)
    ordering = jax.random.permutation(jax.random.fold_in(key, 1), N_PEER - 2) + 1
    positions = jnp.arange(ROUNDS_DEV * N_GROUP, dtype=jnp.int32) % (N_PEER - 2)
    masks = ordering[positions]
    place = jax.random.randint(jax.random.fold_in(key, 2), (), 0, ROUNDS_DEV * N_GROUP)
    return masks.at[place].set(N_PEER - 1).astype(jnp.int32)


def set_ends(result, key, low, top_value):
    dims = result.shape
    index_at = [jax.random.randint(jax.random.fold_in(key, axis), (), 0, dims[axis]) for axis in range(len(dims))]
    result = result.at[tuple(index_at)].set(low)
    longest = dims.index(max(dims))
    index_at[longest] = (index_at[longest] + 1) % dims[longest]
    return result.at[tuple(index_at)].set(top_value)


def steps_of(key, shape, pieces, low, largest):
    def one(dim, blocks):
        heights = jax.random.uniform(jax.random.fold_in(jax.random.fold_in(key, 6), dim), (blocks,), jnp.float32, low / len(pieces), largest / len(pieces))
        return jnp.repeat(jnp.exp(heights), shape[dim] // blocks).reshape((-1,) + (1,) * (len(shape) - dim - 1))

    loudness = one(*pieces[0])
    for cut in pieces[1:]:
        loudness = loudness * one(*cut)
    return loudness


def noise(key, dims, width, bound, shards=(), kind=jnp.bfloat16):
    entries = jax.random.normal(key, dims, jnp.float32) * width
    if len(shards) > 0:
        entries = steps_of(key, dims, shards, -0.22, 0.18) * entries
    return jnp.clip(entries, min=-bound, max=bound).astype(kind)


def setup_inputs(seed: int = 0) -> dict:
    splits = jax.random.split(jax.random.key(seed), 8)
    view_descriptors = noise(splits[0], (CROPS, D), 1.0, 6.0, ((0, 8),))
    embedding_matrix = noise(splits[1], (D, D), D ** -0.5, 0.15625)
    picture_of_view = set_ends(jax.random.randint(splits[2], (CROPS,), 0, 16 * ROWS), jax.random.fold_in(splits[2], 1), 0, (16 * ROWS) - 1).astype(jnp.int32)
    filled_view_places = draw_filled_view_places(jax.random.fold_in(splits[7], 71), 0)
    companion_masks = draw_companion_masks(jax.random.fold_in(splits[7], 71), 0)
    score_scale = jnp.clip(jnp.exp(jax.random.uniform(splits[5], (1,), jnp.float32, math.log(4.0), math.log(16.0))), 4.0, 16.0)
    score_shift = jnp.clip(jax.random.uniform(splits[6], (1,), jnp.float32, -4.0, -1.0), -4.0, -1.0)
    return dict(view_descriptors=view_descriptors, embedding_matrix=embedding_matrix, picture_of_view=picture_of_view, filled_view_places=filled_view_places, companion_masks=companion_masks, score_scale=score_scale, score_shift=score_shift)


def project(view_descriptors, embedding_matrix):
    raw = jnp.dot(view_descriptors, embedding_matrix, preferred_element_type=jnp.float32)
    row_length = jnp.sqrt(lax.optimization_barrier(jnp.sum(raw * raw, axis=1, keepdims=True)) + 1e-06)
    return (raw / row_length, row_length)

def square_extent(self_reduced_vectors, self_identities, views_per_device, companion_normed_part, remote_identities, companion_views, scale_scalar, shift_scalar):
    similarity_matrix = lax.dot_general(self_reduced_vectors, companion_normed_part, (((1,), (1,)), ((), ())), preferred_element_type=jnp.float32)
    row_image_index = jnp.arange(self_reduced_vectors.shape[0], dtype=jnp.int32)
    col_ids = jnp.arange(companion_normed_part.shape[0], dtype=jnp.int32)
    valid_flags = (row_image_index[:, None] < views_per_device) & (col_ids[None, :] < companion_views)
    target_signs = jnp.where(self_identities[:, None] == remote_identities[None, :], 1.0, -1.0).astype(jnp.float32)
    multiplied_scores = scale_scalar * similarity_matrix + shift_scalar
    couple_penalty = jnp.sum(jnp.where(valid_flags, jax.nn.softplus(-target_signs * multiplied_scores), 0.0))
    sigmoid_derivatives = jnp.where(valid_flags, -target_signs * jax.nn.sigmoid(-target_signs * multiplied_scores) * scale_scalar, 0.0).astype(jnp.bfloat16)
    return (couple_penalty, jnp.dot(sigmoid_derivatives, companion_normed_part, preferred_element_type=jnp.float32))

def block_grad(operands):
    return lax.dot_general(operands[0], operands[1], (((0,), (0,)), ((), ())), preferred_element_type=jnp.float32)

def reference(view_descriptors, embedding_matrix, picture_of_view, filled_view_places, companion_masks, score_scale, score_shift):
    unit_rows, row_length = project(view_descriptors, embedding_matrix)
    group_matrices = unit_rows.astype(jnp.bfloat16).reshape(N_PEER, ROWS, D)
    identity_groups = picture_of_view.reshape(N_PEER, ROWS)
    scale_scalar = score_scale[0]
    shift_scalar = score_shift[0]
    seat_ids = jnp.arange(N_PEER, dtype=jnp.int32)
    matched_flags = jax.vmap(square_extent, in_axes=(0, 0, 0, 0, 0, 0, None, None))
    dunit = jnp.zeros((N_PEER, ROWS, D), jnp.float32)
    losses = []
    for member in range(N_GROUP):
        running = jnp.zeros((N_PEER,), jnp.float32)
        for turn_number in range(ROUNDS_DEV):
            companion_member = jnp.bitwise_xor(seat_ids, companion_masks[member * ROUNDS_DEV + turn_number]).astype(jnp.int32)
            couple_penalty, derivative_matrix = matched_flags(group_matrices, identity_groups, filled_view_places, group_matrices[companion_member], identity_groups[companion_member], filled_view_places[companion_member], scale_scalar, shift_scalar)
            running = running + couple_penalty
            dunit = dunit + derivative_matrix
        losses.append(running)
    block_loss = jnp.stack(losses, axis=1) / (ROWS * ROWS)
    flat = dunit.reshape(N_PEER * ROWS, D)
    tangent = (flat - unit_rows * lax.optimization_barrier(jnp.sum(unit_rows * flat, axis=1, keepdims=True))) / row_length
    grad_blocks = tangent.astype(jnp.bfloat16).reshape(N_PEER, ROWS, D)
    feat_blocks = view_descriptors.reshape(N_PEER, ROWS, D)
    grads = lax.map(block_grad, (feat_blocks, grad_blocks))
    return (grads.reshape(N_PEER * D, D), block_loss)
```

```python
import jax
import jax.numpy as jnp
from jax import lax
from jax.sharding import PartitionSpec as P


def swap(block, axis, mask):
    count = lax.axis_size(axis)
    return lax.ppermute(block, axis, [(i, i ^ mask) for i in range(count)])


def project(view_descriptors, embedding_matrix):
    raw = jnp.dot(view_descriptors, embedding_matrix, preferred_element_type=jnp.float32)
    row_length = jnp.sqrt(jnp.sum(raw * raw, axis=1, keepdims=True) + 1e-06)
    return (raw / row_length, row_length)


def pair_terms(scores, ids_here, ids_there, used_here, used_there, scale, shift):
    used = used_here[:, None, None] & used_there[None]
    signs = jnp.where(ids_here[:, None, None] == ids_there[None], 1.0, -1.0).astype(jnp.float32)
    logits = scale * scores + shift
    penalties = jnp.where(used, jax.nn.softplus(-signs * logits), 0.0)
    slopes = jnp.where(used, -signs * jax.nn.sigmoid(-signs * logits) * scale, 0.0)
    return (penalties, slopes.astype(jnp.bfloat16))


def scatter_sum(block):
    count = lax.axis_size("group")
    me = lax.axis_index("group")
    rows, columns = block.shape
    block = block.reshape(rows, count, columns // count)
    kept = count
    for bit in range(count.bit_length() - 1):
        mine = jnp.bitwise_and(jnp.right_shift(me, bit), 1)
        pairs = block.reshape(rows, kept // 2, 2, -1)
        keep = lax.dynamic_index_in_dim(pairs, mine, 2, keepdims=False)
        send = lax.dynamic_index_in_dim(pairs, 1 - mine, 2, keepdims=False)
        if bit > 0:
            send = send.astype(jnp.bfloat16)
        block = keep + swap(send, "group", 1 << bit).astype(jnp.float32)
        kept //= 2
    return block.reshape(rows, columns // count)


def gather_quarters(part):
    far = [swap(part, "peer", m) for m in (6, 4, 2)]
    near = swap(part, "peer", 1)
    crossed = [swap(block, "peer", 1) for block in far]
    return [near, far[2], crossed[2], far[1], crossed[1], far[0], crossed[0]]


def small_plan(
    view_descriptors, embedding_matrix, picture_of_view, filled, companion_masks, scale, shift
):
    rows, width = view_descriptors.shape
    members = lax.axis_size("group")
    me, g = lax.axis_index("peer"), lax.axis_index("group")
    size = rows // members
    begin = g * size
    part_ids = lax.dynamic_slice(picture_of_view, (begin,), (size,))
    facts = lax.all_gather(
        jnp.concatenate([part_ids, filled, companion_masks]), ("peer", "group")
    ).reshape(lax.axis_size("peer"), members, size + 2)
    part = lax.dynamic_slice(view_descriptors, (begin, 0), (size, width))
    part_unit = project(part, embedding_matrix)[0].astype(jnp.bfloat16)
    blocks = jnp.stack(gather_quarters(part_unit))
    unit_rows, row_length = project(view_descriptors, embedding_matrix)
    unit_bf = unit_rows.astype(jnp.bfloat16)

    masks = facts[0, :, size + 1]
    partners = jnp.bitwise_xor(me, masks)
    theirs = facts[partners, g]
    used_there = begin + jnp.arange(size, dtype=jnp.int32)[None] < theirs[:, size, None]
    used_here = jnp.arange(rows, dtype=jnp.int32) < filled[0]
    chosen = blocks[masks - 1].reshape(members * size, width)
    scores = lax.dot_general(
        unit_bf, chosen, (((1,), (1,)), ((), ())), preferred_element_type=jnp.float32
    )
    penalties, slopes = pair_terms(
        scores.reshape(rows, members, size),
        picture_of_view,
        theirs[:, :size],
        used_here,
        used_there,
        scale,
        shift,
    )
    losses = lax.psum(jnp.sum(penalties, axis=(0, 2)), "group")
    dunit = jnp.dot(
        slopes.reshape(rows, members * size), chosen, preferred_element_type=jnp.float32
    )
    return (unit_rows, row_length, dunit, losses[g])


def large_plan(
    view_descriptors, embedding_matrix, picture_of_view, filled, companion_masks, scale, shift
):
    rows = view_descriptors.shape[0]
    unit_rows, row_length = project(view_descriptors, embedding_matrix)
    unit_bf = unit_rows.astype(jnp.bfloat16)
    current = (unit_bf, picture_of_view, filled)
    for bit in range(lax.axis_size("peer").bit_length() - 1):
        arrived = [swap(value, "peer", 1 << bit) for value in current]
        chosen = jnp.bitwise_and(jnp.right_shift(companion_masks[0], bit), 1) == 1
        current = [jnp.where(chosen, new, old) for new, old in zip(arrived, current)]
    theirs, their_ids, their_filled = current
    scores = lax.dot_general(
        unit_bf, theirs, (((1,), (1,)), ((), ())), preferred_element_type=jnp.float32
    )
    index = jnp.arange(rows, dtype=jnp.int32)
    penalties, slopes = pair_terms(
        scores[:, None],
        picture_of_view,
        their_ids[None],
        index < filled[0],
        (index < their_filled[0])[None],
        scale,
        shift,
    )
    dunit = jnp.dot(slopes[:, 0], theirs, preferred_element_type=jnp.float32)
    return (unit_rows, row_length, dunit, jnp.sum(penalties))


def on_device(
    view_descriptors,
    embedding_matrix,
    picture_of_view,
    filled_view_places,
    companion_masks,
    score_scale,
    score_shift,
):
    rows = view_descriptors.shape[0]
    plan = small_plan if lax.axis_size("peer") == 8 else large_plan
    unit_rows, row_length, dunit, loss = plan(
        view_descriptors,
        embedding_matrix,
        picture_of_view,
        filled_view_places,
        companion_masks,
        score_scale[0],
        score_shift[0],
    )
    tangent = (
        dunit - unit_rows * jnp.sum(unit_rows * dunit, axis=1, keepdims=True)
    ) / row_length
    draw = scatter_sum(tangent).astype(jnp.bfloat16)
    projector_grad = lax.dot_general(
        view_descriptors, draw, (((0,), (0,)), ((), ())), preferred_element_type=jnp.float32
    )
    return (projector_grad, (loss / (rows * rows)).reshape(1, 1))


def solution(mesh):
    placed = (P("peer", None), P(), P("peer"), P("peer"), P("group"), P(), P())
    return jax.shard_map(
        on_device,
        mesh=mesh,
        in_specs=placed,
        out_specs=(P("peer", "group"), P("peer", "group")),
        check_vma=False,
    )
```

```python
import functools

import jax
import jax.numpy as jnp
from jax import lax
from jax.experimental import pallas as pl
from jax.experimental.pallas import tpu as pltpu
from jax.sharding import PartitionSpec as P

AXES = ("peer", "group")
FIRST = 128
VMEM = pl.BlockSpec(memory_space=pltpu.VMEM)
SMEM = pl.BlockSpec(memory_space=pltpu.SMEM)


def swap(block, axis, mask):
    count = lax.axis_size(axis)
    return lax.ppermute(block, axis, [(i, i ^ mask) for i in range(count)])


def swap_cores(block, even_mask, odd_mask):
    members = lax.axis_size("group")
    route = []
    for p in range(lax.axis_size("peer")):
        for g in range(members):
            mask = (even_mask, odd_mask)[g & 1]
            if mask is not None:
                route.append((p * members + g, (p ^ mask) * members + g))
    return lax.ppermute(block, AXES, route)


def project(view_descriptors, embedding_matrix):
    raw = jnp.dot(view_descriptors, embedding_matrix, preferred_element_type=jnp.float32)
    row_length = jnp.sqrt(jnp.sum(raw * raw, axis=1, keepdims=True) + 1e-06)
    return (raw / row_length, row_length)


def half_unit_kernel(half_ref, features, matrix, unit, raw, squares):
    step = pl.program_id(0)
    block = jnp.dot(features[...], matrix[...], preferred_element_type=jnp.float32)
    raw[step] = block
    partial = jnp.sum(block * block, axis=1, keepdims=True)

    @pl.when(step == 0)
    def _():
        squares[...] = jnp.broadcast_to(partial, squares.shape)

    @pl.when(step > 0)
    def _():
        squares[...] += partial

    @pl.when(step == pl.num_programs(0) - 1)
    def _():
        length = jnp.sqrt(squares[...][:, :1] + 1e-06)
        width = block.shape[1]
        for k in range(raw.shape[0]):
            unit[:, k * width : (k + 1) * width] = (raw[k] / length).astype(jnp.bfloat16)


def half_unit(half, features, matrix):
    rows, depth = features.shape
    width = matrix.shape[1]
    steps = 4
    return pl.pallas_call(
        half_unit_kernel,
        out_shape=jax.ShapeDtypeStruct((rows // 2, width), jnp.bfloat16),
        grid_spec=pltpu.PrefetchScalarGridSpec(
            num_scalar_prefetch=1,
            grid=(steps,),
            in_specs=[
                pl.BlockSpec((rows // 2, depth), lambda j, h: (h[0], 0)),
                pl.BlockSpec((depth, width // steps), lambda j, h: (0, j)),
            ],
            out_specs=pl.BlockSpec((rows // 2, width), lambda j, h: (0, 0)),
            scratch_shapes=[
                pltpu.VMEM((steps, rows // 2, width // steps), jnp.float32),
                pltpu.VMEM((rows // 2, 128), jnp.float32),
            ],
        ),
        compiler_params=pltpu.CompilerParams(vmem_limit_bytes=24 << 20),
        cost_estimate=pl.CostEstimate(
            flops=rows * depth * width, bytes_accessed=2 * depth * width, transcendentals=0
        ),
        name="half_unit",
    )(half, features, matrix)


def pair_kernel(cuts, first, final, *refs):
    refs = list(refs)
    numbers, factors, ids_here, unit_bf = refs[:4]
    del refs[:4]
    blocks = [refs.pop(0) for _ in cuts]
    ids_there = [refs.pop(0) for _ in cuts]
    if not first:
        old_dunit, old_losses = refs.pop(0), refs.pop(0)
    if final:
        unit, length = refs.pop(0), refs.pop(0)
        keep, send, stacked, total = refs
    else:
        total, losses_out, stacked = refs
    scale, shift = factors[0], factors[1]
    rows = unit_bf.shape[0]
    offset = 0
    for block, (_, begin, count) in zip(blocks, cuts):
        stacked[offset : offset + count] = block[...]
        offset += count
    scores = lax.dot_general(
        unit_bf[...], stacked[...], (((1,), (1,)), ((), ())), preferred_element_type=jnp.float32
    )
    row = lax.broadcasted_iota(jnp.int32, (rows, 1), 0)
    used_here = row < numbers[0]
    lane = lax.broadcasted_iota(jnp.int32, (1, 128), 1)
    losses = jnp.zeros((1, 128), jnp.float32) if first else old_losses[0:1]
    slopes = []
    offset = 0
    for (slot, begin, count), ids in zip(cuts, ids_there):
        turn, filled = numbers[2 + slot], numbers[6 + slot]
        place = numbers[1] + begin + lax.broadcasted_iota(jnp.int32, (1, count), 1)
        used = used_here & (place < filled) & (turn >= 0)
        signs = jnp.where(ids_here[...] == ids[...], -1.0, 1.0)
        logits = signs * (scale * scores[:, offset : offset + count] + shift)
        small = jnp.exp(-jnp.abs(logits))
        penalty = jnp.maximum(logits, 0.0) + jnp.log1p(small)
        loss = jnp.sum(jnp.where(used, penalty, 0.0))
        losses = losses + jnp.where(lane == turn, loss, 0.0)
        gate = jnp.where(logits >= 0, 1.0, small) / (1.0 + small)
        slopes.append(jnp.where(used, signs * gate * scale, 0.0).astype(jnp.bfloat16))
        offset += count
    slopes = slopes[0] if len(slopes) == 1 else jnp.concatenate(slopes, axis=1)
    width = stacked.shape[1]
    step = width // 4
    for k in range(4):
        at = slice(k * step, (k + 1) * step)
        part = jnp.dot(slopes, stacked[:, at], preferred_element_type=jnp.float32)
        total[:, at] = part if first else old_dunit[:, at] + part
    if not final:
        losses_out[...] = jnp.broadcast_to(losses, losses_out.shape)
        return
    along = jnp.sum(unit[...] * total[...], axis=1, keepdims=True)
    total[...] = (total[...] - unit[...] * along) / length[...]
    me = numbers[10]
    for k, other in enumerate((0, 2)):
        at = pl.ds(pl.multiple_of(jnp.bitwise_xor(me, other) * step, 128), step)
        keep[:rows, k * step : (k + 1) * step] = total[:, at]
        at = pl.ds(pl.multiple_of(jnp.bitwise_xor(me, other + 1) * step, 128), step)
        send[:rows, k * step : (k + 1) * step] = total[:, at]
    keep[rows:, :] = jnp.zeros((8, 2 * step), jnp.float32)
    keep[rows : rows + 1, 0:128] = losses
    send[rows:, :] = jnp.zeros((8, 2 * step), jnp.float32)
    send[rows : rows + 1, 0:128] = losses


def pair_terms(numbers, factors, ids_here, unit_bf, blocks, ids_there, cuts, old=None, final=None):
    rows, width = unit_bf.shape
    total = sum(count for _, _, count in cuts)
    args = [numbers, factors, ids_here, unit_bf, *blocks, *ids_there]
    scratch = [pltpu.VMEM((total, width), jnp.bfloat16)]
    if old is not None:
        args += old
    if final is not None:
        args += final
        shapes = [jax.ShapeDtypeStruct((rows + 8, width // 2), jnp.float32)] * 2
        scratch += [pltpu.VMEM((rows, width), jnp.float32)]
    else:
        shapes = [
            jax.ShapeDtypeStruct((rows, width), jnp.float32),
            jax.ShapeDtypeStruct((8, 128), jnp.float32),
        ]
    return pl.pallas_call(
        functools.partial(pair_kernel, cuts, old is None, final is not None),
        out_shape=shapes,
        in_specs=[SMEM, SMEM] + [VMEM] * (len(args) - 2),
        out_specs=[VMEM] * 2,
        scratch_shapes=scratch,
        compiler_params=pltpu.CompilerParams(vmem_limit_bytes=32 << 20),
        cost_estimate=pl.CostEstimate(
            flops=4 * rows * width * total,
            bytes_accessed=8 * rows * width,
            transcendentals=3 * rows * total,
        ),
        name="pair_terms",
    )(*args)


def combine_kernel(keep, arrived, own, send):
    rows, step = own.shape[0] - 8, own.shape[1]
    own[...] = keep[:, :step] + arrived[:, :step]
    send[:rows] = (keep[:rows, step:] + arrived[:rows, step:]).astype(jnp.bfloat16)
    losses = keep[rows : rows + 1, 0:128] + arrived[rows : rows + 1, 0:128]
    high = losses.astype(jnp.bfloat16).astype(jnp.float32)
    middle = (losses - high).astype(jnp.bfloat16).astype(jnp.float32)
    low = losses - high - middle
    line = lax.broadcasted_iota(jnp.int32, (16, 128), 0)
    packed = jnp.where(line == 0, high, jnp.where(line == 1, middle, jnp.where(line == 2, low, 0.0)))
    send[rows:] = jnp.zeros((16, step), jnp.bfloat16)
    send[rows:, 0:128] = packed.astype(jnp.bfloat16)


def combine(keep, arrived):
    rows, width = keep.shape[0] - 8, keep.shape[1]
    return pl.pallas_call(
        combine_kernel,
        out_shape=[
            jax.ShapeDtypeStruct((rows + 8, width // 2), jnp.float32),
            jax.ShapeDtypeStruct((rows + 16, width // 2), jnp.bfloat16),
        ],
        in_specs=[VMEM] * 2,
        out_specs=[VMEM] * 2,
        compiler_params=pltpu.CompilerParams(vmem_limit_bytes=16 << 20),
        name="combine",
    )(keep, arrived)


def gradient_kernel(me, own, arrived, features, grad, loss, draw):
    rows = features.shape[1]

    @pl.when(pl.program_id(0) == 0)
    def _():
        draw[...] = (own[:rows] + arrived[:rows].astype(jnp.float32)).astype(jnp.bfloat16)
        parts = arrived[rows:, 0:128].astype(jnp.float32)
        total = own[rows : rows + 1, 0:128] + jnp.sum(parts, axis=0, keepdims=True)
        lane = lax.broadcasted_iota(jnp.int32, (1, 128), 1)
        value = jnp.sum(jnp.where(lane == me[0], total, 0.0))
        loss[0, 0] = value / (rows * rows)

    grad[...] = jnp.dot(features[...], draw[...], preferred_element_type=jnp.float32)


def gradient(me, own, arrived, features_t):
    depth, rows = features_t.shape
    width = own.shape[1]
    steps = 4
    return pl.pallas_call(
        gradient_kernel,
        out_shape=[
            jax.ShapeDtypeStruct((depth, width), jnp.float32),
            jax.ShapeDtypeStruct((1, 1), jnp.float32),
        ],
        grid=(steps,),
        in_specs=[
            SMEM,
            pl.BlockSpec(own.shape, lambda i: (0, 0)),
            pl.BlockSpec(arrived.shape, lambda i: (0, 0)),
            pl.BlockSpec((depth // steps, rows), lambda i: (i, 0)),
        ],
        out_specs=[pl.BlockSpec((depth // steps, width), lambda i: (i, 0)), SMEM],
        scratch_shapes=[pltpu.VMEM((rows, width), jnp.bfloat16)],
        compiler_params=pltpu.CompilerParams(vmem_limit_bytes=16 << 20),
        name="gradient",
    )(me, own, arrived, features_t)


def small_plan(features, matrix, ids, filled, mask, scale, shift):
    rows = features.shape[0]
    half_rows = rows // 2
    me = lax.axis_index("group")
    y, core = me // 2, me % 2

    half = half_unit(y.reshape(1), features, matrix)
    near = swap_cores(half, 1, 2)
    far_a = swap_cores(half[:FIRST], 4, 6)
    far_b = swap_cores(half[FIRST:], 4, 6)
    near_x = swap_cores(near, None, 1)
    far_ax = swap_cores(far_a, 1, 1)
    far_bx = swap_cores(far_b, 1, 1)

    facts = jnp.concatenate([lax.dynamic_slice(ids, (y * half_rows,), (half_rows,)), filled])
    slots = [
        swap_cores(facts, 1, 2),
        swap_cores(facts, None, 3),
        swap_cores(facts, 4, 6),
        swap_cores(facts, 5, 7),
    ]
    two = jnp.stack([mask[0], swap(mask, "group", 1)[0]])
    other_two = swap(two, "group", 2)
    pair = jnp.arange(4, dtype=jnp.int32)
    four = jnp.concatenate([two, other_two])
    slot_masks = jnp.where(core == 0, jnp.array([1, 0, 4, 5]), jnp.array([2, 3, 6, 7]))
    hit = four[None, :] == slot_masks[:, None]
    turns = jnp.max(jnp.where(hit, jnp.bitwise_xor(pair, me)[None, :], -1), axis=1)
    counts = jnp.stack([slot[half_rows] for slot in slots])
    numbers = jnp.concatenate(
        [filled, (y * half_rows).reshape(1), turns, counts, me.reshape(1)]
    ).astype(jnp.int32)
    factors = jnp.stack([scale, shift])
    there = [slot[None, :half_rows] for slot in slots]
    ids_here = ids[:, None]

    unit, length = project(features, matrix)
    unit_bf = unit.astype(jnp.bfloat16)
    common = (numbers, factors, ids_here, unit_bf)
    early = pair_terms(
        *common, [near, near_x], there[:2], ((0, 0, half_rows), (1, 0, half_rows))
    )
    middle = pair_terms(
        *common,
        [far_a, far_ax],
        [there[2][:, :FIRST], there[3][:, :FIRST]],
        ((2, 0, FIRST), (3, 0, FIRST)),
        old=early,
    )
    rest = half_rows - FIRST
    keep, send = pair_terms(
        *common,
        [far_b, far_bx],
        [there[2][:, FIRST:], there[3][:, FIRST:]],
        ((2, FIRST, rest), (3, FIRST, rest)),
        old=middle,
        final=[unit, length],
    )
    own, send = combine(keep, swap(send, "group", 1))
    return gradient(me.reshape(1), own, swap(send, "group", 2), features.T)


def scatter_sum(block):
    count = lax.axis_size("group")
    me = lax.axis_index("group")
    rows, columns = block.shape
    block = block.reshape(rows, count, columns // count)
    kept = count
    for bit in range(count.bit_length() - 1):
        mine = jnp.bitwise_and(jnp.right_shift(me, bit), 1)
        pairs = block.reshape(rows, kept // 2, 2, -1)
        keep = lax.dynamic_index_in_dim(pairs, mine, 2, keepdims=False)
        send = lax.dynamic_index_in_dim(pairs, 1 - mine, 2, keepdims=False)
        if bit > 0:
            send = send.astype(jnp.bfloat16)
        block = keep + swap(send, "group", 1 << bit).astype(jnp.float32)
        kept //= 2
    return block.reshape(rows, columns // count)


def large_plan(features, matrix, ids, filled, mask, scale, shift):
    rows = features.shape[0]
    unit, length = project(features, matrix)
    unit_bf = unit.astype(jnp.bfloat16)
    current = (unit_bf, ids, filled)
    for bit in range(lax.axis_size("peer").bit_length() - 1):
        arrived = [swap(value, "peer", 1 << bit) for value in current]
        chosen = jnp.bitwise_and(jnp.right_shift(mask[0], bit), 1) == 1
        current = [jnp.where(chosen, new, old) for new, old in zip(arrived, current)]
    theirs, their_ids, their_filled = current
    scores = lax.dot_general(
        unit_bf, theirs, (((1,), (1,)), ((), ())), preferred_element_type=jnp.float32
    )
    index = jnp.arange(rows, dtype=jnp.int32)
    used = (index < filled[0])[:, None] & (index < their_filled[0])[None]
    signs = jnp.where(ids[:, None] == their_ids[None], 1.0, -1.0).astype(jnp.float32)
    logits = scale * scores + shift
    loss = jnp.sum(jnp.where(used, jax.nn.softplus(-signs * logits), 0.0))
    slopes = jnp.where(used, -signs * jax.nn.sigmoid(-signs * logits) * scale, 0.0)
    dunit = jnp.dot(slopes.astype(jnp.bfloat16), theirs, preferred_element_type=jnp.float32)
    tangent = (dunit - unit * jnp.sum(unit * dunit, axis=1, keepdims=True)) / length
    draw = scatter_sum(tangent).astype(jnp.bfloat16)
    grad = lax.dot_general(
        features, draw, (((0,), (0,)), ((), ())), preferred_element_type=jnp.float32
    )
    return (grad, (loss / (rows * rows)).reshape(1, 1))


def on_device(
    view_descriptors,
    embedding_matrix,
    picture_of_view,
    filled_view_places,
    companion_masks,
    score_scale,
    score_shift,
):
    small = lax.axis_size("peer") == 8 and lax.axis_size("group") == 4
    plan = small_plan if small else large_plan
    return plan(
        view_descriptors,
        embedding_matrix,
        picture_of_view,
        filled_view_places,
        companion_masks,
        score_scale[0],
        score_shift[0],
    )


def solution(mesh):
    placed = (P("peer", None), P(), P("peer"), P("peer"), P("group"), P(), P())
    return jax.shard_map(
        on_device,
        mesh=mesh,
        in_specs=placed,
        out_specs=(P("peer", "group"), P("peer", "group")),
        check_vma=False,
    )
```

```python
import functools

import jax
import jax.numpy as jnp
from jax import lax
from jax.experimental import pallas as pl
from jax.experimental.pallas import tpu as pltpu
from jax.sharding import PartitionSpec as P

AXES = ("peer", "group")
FIRST = 112
SLOTS = ((1, 2, 3, 4, 5), (1, 2, 3, 6, 7))
STEPS = 6
SMALL = pl.CostEstimate(flops=1, bytes_accessed=1, transcendentals=0)
ANY = pl.BlockSpec(memory_space=pl.ANY)
VMEM = pl.BlockSpec(memory_space=pltpu.VMEM)
SMEM = pl.BlockSpec(memory_space=pltpu.SMEM)


def swap(block, axis, mask):
    count = lax.axis_size(axis)
    return lax.ppermute(block, axis, [(i, i ^ mask) for i in range(count)])


def swap_cores(block, even_mask, odd_mask):
    members = lax.axis_size("group")
    route = []
    for p in range(lax.axis_size("peer")):
        for g in range(members):
            mask = (even_mask, odd_mask)[g & 1]
            if mask is not None:
                route.append((p * members + g, (p ^ mask) * members + g))
    return lax.ppermute(block, AXES, route)


def project(view_descriptors, embedding_matrix):
    raw = jnp.dot(view_descriptors, embedding_matrix, preferred_element_type=jnp.float32)
    row_length = jnp.sqrt(jnp.sum(raw * raw, axis=1, keepdims=True) + 1e-06)
    return (raw / row_length, row_length)


def after(value, *others):
    return lax.optimization_barrier((value, *others))[0]


def load(features, matrix, features_v, matrix_v, sems, begin, rows):
    depth = matrix_v.shape[0] // STEPS
    copies = [pltpu.make_async_copy(features.at[pl.ds(begin, rows)], features_v, sems.at[STEPS])]
    for k in range(STEPS):
        at = pl.ds(k * depth, depth)
        copies.append(pltpu.make_async_copy(matrix.at[at], matrix_v.at[at], sems.at[k]))
    for copy in copies:
        copy.start()
    return copies


def multiply(copies, features_v, matrix_v, raw):
    depth = matrix_v.shape[0] // STEPS
    copies[0].wait()
    for k in range(STEPS):
        at = slice(k * depth, (k + 1) * depth)
        copies[1 + k].wait()
        part = jnp.dot(features_v[:, at], matrix_v[at], preferred_element_type=jnp.float32)
        raw[...] = part if k == 0 else raw[...] + part
    return jnp.sqrt(jnp.sum(raw[...] * raw[...], axis=1, keepdims=True) + 1e-06)


def half_unit_kernel(ids, filled, features, matrix, unit, unit_a, unit_b, features_v, matrix_v, raw, sems):
    me = lax.axis_index("group")
    y, core = me // 2, me % 2
    half = raw.shape[0]
    first = unit_a.shape[0] - 16
    copies = load(features, matrix, features_v, matrix_v, sems, y * half, half)
    row_ids = ids[...].reshape(1, 2 * half)
    row_ids = jnp.where(y == 0, row_ids[:, :half], row_ids[:, half:])
    part_ids = jnp.where(core == 0, row_ids[:, : half // 2], row_ids[:, half // 2 :])
    count = jnp.full((1, 256), filled[0], jnp.int32)
    row = lax.broadcasted_iota(jnp.int32, (16, 1024), 0)
    for out, value in ((unit, part_ids), (unit_a, row_ids)):
        digits = []
        for number in (value, count):
            missing = 256 - number.shape[1]
            for digit in (number & 255, number >> 8):
                digits.append(digit.astype(jnp.float32))
                if missing:
                    digits.append(jnp.zeros((1, missing), jnp.float32))
        facts = jnp.where(row == 0, jnp.concatenate(digits, axis=1), 0.0).astype(jnp.bfloat16)
        begin = out.shape[0] - 16
        out[begin:] = jnp.zeros((16, out.shape[1]), jnp.bfloat16)
        out[begin:, :1024] = facts
    length = multiply(copies, features_v, matrix_v, raw)
    value = (raw[...] / length).astype(jnp.bfloat16)
    unit[: half // 2] = jnp.where(core == 0, value[: half // 2], value[half // 2 :])
    unit_a[:first] = value[:first]
    unit_b[...] = value[first:]


def half_unit(ids, filled, features, matrix, first):
    rows, depth = features.shape
    width = matrix.shape[1]
    half = rows // 2
    return pl.pallas_call(
        half_unit_kernel,
        out_shape=[
            jax.ShapeDtypeStruct((count, width), jnp.bfloat16)
            for count in (half // 2 + 16, first + 16, half - first)
        ],
        in_specs=[VMEM, SMEM, ANY, ANY],
        out_specs=[VMEM] * 3,
        scratch_shapes=[
            pltpu.VMEM((half, depth), jnp.bfloat16),
            pltpu.VMEM((depth, width), jnp.bfloat16),
            pltpu.VMEM((half, width), jnp.float32),
            pltpu.SemaphoreType.DMA((STEPS + 1,)),
        ],
        compiler_params=pltpu.CompilerParams(vmem_limit_bytes=60 << 20),
        cost_estimate=pl.CostEstimate(flops=rows * depth * width, bytes_accessed=2 * depth * width, transcendentals=0),
        name="half_unit",
    )(ids, filled, features, matrix)


def whole_unit_kernel(ids, features, matrix, unit, unit_bf, length, column, features_v, matrix_v, sems):
    rows = unit.shape[0]
    copies = load(features, matrix, features_v, matrix_v, sems, 0, rows)
    column[...] = jnp.broadcast_to(ids[...].reshape(1, rows).astype(jnp.float32), (128, rows)).T
    norm = multiply(copies, features_v, matrix_v, unit)
    length[...] = jnp.broadcast_to(norm, length.shape)
    unit[...] = unit[...] / norm
    unit_bf[...] = unit[...].astype(jnp.bfloat16)


def whole_unit(ids, features, matrix):
    rows, depth = features.shape
    width = matrix.shape[1]
    return pl.pallas_call(
        whole_unit_kernel,
        out_shape=[
            jax.ShapeDtypeStruct((rows, width), jnp.float32),
            jax.ShapeDtypeStruct((rows, width), jnp.bfloat16),
            jax.ShapeDtypeStruct((rows, 128), jnp.float32),
            jax.ShapeDtypeStruct((rows, 128), jnp.float32),
        ],
        in_specs=[VMEM, ANY, ANY],
        out_specs=[VMEM] * 4,
        scratch_shapes=[
            pltpu.VMEM((rows, depth), jnp.bfloat16),
            pltpu.VMEM((depth, width), jnp.bfloat16),
            pltpu.SemaphoreType.DMA((STEPS + 1,)),
        ],
        compiler_params=pltpu.CompilerParams(vmem_limit_bytes=28 << 20),
        cost_estimate=pl.CostEstimate(flops=2 * rows * depth * width, bytes_accessed=4 * depth * width, transcendentals=0),
        name="whole_unit",
    )(ids, features, matrix)


def pair_kernel(cuts, first, final, *refs):
    refs = list(refs)
    masks = refs[:4]
    scale, shift, filled_here = refs[4][0], refs[5][0], refs[6][0]
    ids_here, unit_bf = refs[7:9]
    del refs[:9]
    blocks = [refs.pop(0) for _ in cuts]
    if not first:
        old_dunit, old_losses = refs.pop(0), refs.pop(0)
    if final:
        old_facts, unit, length = refs.pop(0), refs.pop(0), refs.pop(0)
        keep, send, stacked, total = refs
    else:
        total, losses_out, facts_out, stacked = refs
    me = lax.axis_index("group")
    y, core = me // 2, me % 2
    rows = unit_bf.shape[0]
    half = rows // 2
    offset = 0
    for block, (_, begin, count) in zip(blocks, cuts):
        stacked[offset : offset + count] = block[:count]
        offset += count
    scores = lax.dot_general(
        unit_bf[...], stacked[...], (((1,), (1,)), ((), ())), preferred_element_type=jnp.float32
    )
    row = lax.broadcasted_iota(jnp.int32, (rows, 1), 0)
    used_here = row < filled_here
    lane = lax.broadcasted_iota(jnp.int32, (1, 128), 1)
    losses = jnp.zeros((1, 128), jnp.float32) if first else old_losses[0:1]
    slopes = []
    offset = 0
    for k, (slot, begin, count) in enumerate(cuts):
        wanted = jnp.where(core == 0, SLOTS[0][slot], SLOTS[1][slot])
        turn = jnp.int32(-1)
        for e, mask in enumerate(masks):
            turn = jnp.where(mask[0] == wanted, jnp.bitwise_xor(me, e), turn)
        if final:
            fact = old_facts[16 * k : 16 * (k + 1)]
        else:
            fact = blocks[k][count : count + 16]
            facts_out[16 * k : 16 * (k + 1)] = fact
        fact = fact.astype(jnp.float32)[0:1]
        ids = fact[:, begin : begin + count] + 256.0 * fact[:, 256 + begin : 256 + begin + count]
        filled = fact[:, 512:513] + 256.0 * fact[:, 768:769]
        base = me * (half // 2) if slot < 3 else y * half + begin
        place = base + lax.broadcasted_iota(jnp.int32, (1, count), 1)
        used = used_here & (place < filled.astype(jnp.int32)) & (turn >= 0)
        signs = jnp.where(ids_here[:, :1] == ids, -1.0, 1.0)
        logits = signs * (scale * scores[:, offset : offset + count] + shift)
        small = jnp.exp(-jnp.abs(logits))
        penalty = jnp.maximum(logits, 0.0) + jnp.log1p(small)
        loss = jnp.sum(jnp.where(used, penalty, 0.0))
        losses = losses + jnp.where(lane == turn, loss, 0.0)
        gate = jnp.where(logits >= 0, 1.0, small) / (1.0 + small)
        slopes.append(jnp.where(used, signs * gate * scale, 0.0).astype(jnp.bfloat16))
        offset += count
    slopes = slopes[0] if len(slopes) == 1 else jnp.concatenate(slopes, axis=1)
    width = stacked.shape[1]
    step = width // 4
    for k in range(4):
        at = slice(k * step, (k + 1) * step)
        part = jnp.dot(slopes, stacked[:, at], preferred_element_type=jnp.float32)
        total[:, at] = part if first else old_dunit[:, at] + part
    if not final:
        losses_out[...] = jnp.broadcast_to(losses, losses_out.shape)
        return
    along = jnp.sum(unit[...] * total[...], axis=1, keepdims=True)
    total[...] = (total[...] - unit[...] * along) / length[:, :1]
    for k, other in enumerate((0, 2)):
        at = pl.ds(pl.multiple_of(jnp.bitwise_xor(me, other) * step, 128), step)
        keep[:rows, k * step : (k + 1) * step] = total[:, at]
        at = pl.ds(pl.multiple_of(jnp.bitwise_xor(me, other + 1) * step, 128), step)
        send[:rows, k * step : (k + 1) * step] = total[:, at]
    keep[rows:, :] = jnp.zeros((8, 2 * step), jnp.float32)
    keep[rows : rows + 1, 0:128] = losses
    send[rows:, :] = jnp.zeros((8, 2 * step), jnp.float32)
    send[rows : rows + 1, 0:128] = losses


def pair_terms(scalars, ids_here, unit_bf, blocks, cuts, old=None, final=None):
    rows, width = unit_bf.shape
    total = sum(count for _, _, count in cuts)
    args = [*scalars, ids_here, unit_bf, *blocks]
    scratch = [pltpu.VMEM((total, width), jnp.bfloat16)]
    if old is not None:
        args += old
    if final is not None:
        args += final
        shapes = [jax.ShapeDtypeStruct((rows + 8, width // 2), jnp.float32)] * 2
        scratch += [pltpu.VMEM((rows, width), jnp.float32)]
    else:
        shapes = [
            jax.ShapeDtypeStruct((rows, width), jnp.float32),
            jax.ShapeDtypeStruct((8, 128), jnp.float32),
            jax.ShapeDtypeStruct((16 * len(blocks), width), jnp.bfloat16),
        ]
    return pl.pallas_call(
        functools.partial(pair_kernel, cuts, old is None, final is not None),
        out_shape=shapes,
        in_specs=[SMEM] * len(scalars) + [VMEM] * (len(args) - len(scalars)),
        out_specs=[VMEM] * len(shapes),
        scratch_shapes=scratch,
        compiler_params=pltpu.CompilerParams(vmem_limit_bytes=28 << 20),
        cost_estimate=pl.CostEstimate(flops=4 * rows * width * total, bytes_accessed=8 * rows * width, transcendentals=3 * rows * total),
        name="pair_terms",
    )(*args)


def combine_kernel(keep, arrived, own, send):
    rows, step = own.shape[0] - 8, own.shape[1]
    own[...] = keep[:, :step] + arrived[:, :step]
    send[:rows] = (keep[:rows, step:] + arrived[:rows, step:]).astype(jnp.bfloat16)
    losses = keep[rows : rows + 1, 0:128] + arrived[rows : rows + 1, 0:128]
    high = losses.astype(jnp.bfloat16).astype(jnp.float32)
    middle = (losses - high).astype(jnp.bfloat16).astype(jnp.float32)
    low = losses - high - middle
    line = lax.broadcasted_iota(jnp.int32, (16, 128), 0)
    packed = jnp.where(line == 0, high, jnp.where(line == 1, middle, jnp.where(line == 2, low, 0.0)))
    send[rows:] = jnp.zeros((16, step), jnp.bfloat16)
    send[rows:, 0:128] = packed.astype(jnp.bfloat16)


def combine(keep, arrived):
    rows, width = keep.shape[0] - 8, keep.shape[1]
    return pl.pallas_call(
        combine_kernel,
        out_shape=[
            jax.ShapeDtypeStruct((rows + 8, width // 2), jnp.float32),
            jax.ShapeDtypeStruct((rows + 16, width // 2), jnp.bfloat16),
        ],
        in_specs=[VMEM] * 2,
        out_specs=[VMEM] * 2,
        compiler_params=pltpu.CompilerParams(vmem_limit_bytes=16 << 20),
        cost_estimate=pl.CostEstimate(flops=rows * width, bytes_accessed=8 * rows * width, transcendentals=0),
        name="combine",
    )(keep, arrived)


def gradient_kernel(me, own, arrived, features, grad, loss, draw):
    rows = features.shape[1]

    @pl.when(pl.program_id(0) == 0)
    def _():
        draw[...] = (own[:rows] + arrived[:rows].astype(jnp.float32)).astype(jnp.bfloat16)
        parts = arrived[rows:, 0:128].astype(jnp.float32)
        total = own[rows : rows + 1, 0:128] + jnp.sum(parts, axis=0, keepdims=True)
        lane = lax.broadcasted_iota(jnp.int32, (1, 128), 1)
        value = jnp.sum(jnp.where(lane == me[0], total, 0.0))
        loss[0, 0] = value / (rows * rows)

    grad[...] = jnp.dot(features[...], draw[...], preferred_element_type=jnp.float32)


def gradient(me, own, arrived, features_t):
    depth, rows = features_t.shape
    width = own.shape[1]
    steps = 4
    return pl.pallas_call(
        gradient_kernel,
        out_shape=[
            jax.ShapeDtypeStruct((depth, width), jnp.float32),
            jax.ShapeDtypeStruct((1, 1), jnp.float32),
        ],
        grid=(steps,),
        in_specs=[
            SMEM,
            pl.BlockSpec(own.shape, lambda i: (0, 0)),
            pl.BlockSpec(arrived.shape, lambda i: (0, 0)),
            pl.BlockSpec((depth // steps, rows), lambda i: (i, 0)),
        ],
        out_specs=[pl.BlockSpec((depth // steps, width), lambda i: (i, 0)), SMEM],
        scratch_shapes=[pltpu.VMEM((rows, width), jnp.bfloat16)],
        compiler_params=pltpu.CompilerParams(vmem_limit_bytes=16 << 20),
        cost_estimate=pl.CostEstimate(flops=2 * rows * depth * width, bytes_accessed=4 * depth * width, transcendentals=0),
        name="gradient",
    )(me, own, arrived, features_t)


def small_plan(features, matrix, ids, filled, mask, scale, shift):
    rows = features.shape[0]
    half_rows = rows // 2
    rest = half_rows - FIRST

    part, half_a, half_b = half_unit(ids, filled, features, matrix, FIRST)
    near = swap_cores(part, 1, 1)
    far_a = swap_cores(half_a, 4, 6)
    side = swap_cores(part, 2, 2)
    unit, unit_bf, length, column = whole_unit(ids, after(features, part), matrix)
    far_b = swap_cores(after(half_b, side), 4, 6)
    side_x = swap_cores(after(side, near, unit_bf), 1, 1)
    other_masks = [swap(after(mask, side), "group", k) for k in (1, 2, 3)]
    far_ax = swap_cores(after(far_a, side_x, *other_masks), 1, 1)

    common = ([mask, *other_masks, scale, shift, filled], column, unit_bf)
    quarter = half_rows // 2
    early = pair_terms(
        *common,
        [near, side, side_x],
        ((0, 0, quarter), (1, 0, quarter), (2, 0, quarter)),
    )
    far_bx = swap_cores(after(far_b, early[1]), 1, 1)
    middle = pair_terms(
        *common, [far_a, far_ax], ((3, 0, FIRST), (4, 0, FIRST)), old=early[:2]
    )
    keep, send = pair_terms(
        *common,
        [far_b, far_bx],
        ((3, FIRST, rest), (4, FIRST, rest)),
        old=middle[:2],
        final=[middle[2], unit, length],
    )
    own, send = combine(keep, swap(send, "group", 1))
    me = lax.axis_index("group")
    return gradient(me.reshape(1), own, swap(send, "group", 2), features.T)


def scatter_sum(block):
    count = lax.axis_size("group")
    me = lax.axis_index("group")
    rows, columns = block.shape
    block = block.reshape(rows, count, columns // count)
    kept = count
    for bit in range(count.bit_length() - 1):
        mine = jnp.bitwise_and(jnp.right_shift(me, bit), 1)
        pairs = block.reshape(rows, kept // 2, 2, -1)
        keep = lax.dynamic_index_in_dim(pairs, mine, 2, keepdims=False)
        send = lax.dynamic_index_in_dim(pairs, 1 - mine, 2, keepdims=False)
        if bit > 0:
            send = send.astype(jnp.bfloat16)
        block = keep + swap(send, "group", 1 << bit).astype(jnp.float32)
        kept //= 2
    return block.reshape(rows, columns // count)


def large_plan(features, matrix, ids, filled, mask, scale, shift):
    rows = features.shape[0]
    unit, length = project(features, matrix)
    unit_bf = unit.astype(jnp.bfloat16)
    current = (unit_bf, ids, filled)
    for bit in range(lax.axis_size("peer").bit_length() - 1):
        arrived = [swap(value, "peer", 1 << bit) for value in current]
        chosen = jnp.bitwise_and(jnp.right_shift(mask[0], bit), 1) == 1
        current = [jnp.where(chosen, new, old) for new, old in zip(arrived, current)]
    theirs, their_ids, their_filled = current
    scores = lax.dot_general(
        unit_bf, theirs, (((1,), (1,)), ((), ())), preferred_element_type=jnp.float32
    )
    index = jnp.arange(rows, dtype=jnp.int32)
    used = (index < filled[0])[:, None] & (index < their_filled[0])[None]
    signs = jnp.where(ids[:, None] == their_ids[None], 1.0, -1.0).astype(jnp.float32)
    logits = scale[0] * scores + shift[0]
    loss = jnp.sum(jnp.where(used, jax.nn.softplus(-signs * logits), 0.0))
    slopes = jnp.where(used, -signs * jax.nn.sigmoid(-signs * logits) * scale[0], 0.0)
    dunit = jnp.dot(slopes.astype(jnp.bfloat16), theirs, preferred_element_type=jnp.float32)
    tangent = (dunit - unit * jnp.sum(unit * dunit, axis=1, keepdims=True)) / length
    draw = scatter_sum(tangent).astype(jnp.bfloat16)
    grad = lax.dot_general(
        features, draw, (((0,), (0,)), ((), ())), preferred_element_type=jnp.float32
    )
    return (grad, (loss / (rows * rows)).reshape(1, 1))


def on_device(
    view_descriptors,
    embedding_matrix,
    picture_of_view,
    filled_view_places,
    companion_masks,
    score_scale,
    score_shift,
):
    small = lax.axis_size("peer") == 8 and lax.axis_size("group") == 4
    plan = small_plan if small else large_plan
    return plan(
        view_descriptors,
        embedding_matrix,
        picture_of_view,
        filled_view_places,
        companion_masks,
        score_scale,
        score_shift,
    )


def solution(mesh):
    placed = (P("peer", None), P(), P("peer"), P("peer"), P("group"), P(), P())
    return jax.shard_map(
        on_device,
        mesh=mesh,
        in_specs=placed,
        out_specs=(P("peer", "group"), P("peer", "group")),
        check_vma=False,
    )
```

```python
import functools

import jax
import jax.numpy as jnp
from jax import lax
from jax.experimental import pallas as pl
from jax.experimental.pallas import tpu as pltpu
from jax.sharding import PartitionSpec as P

AXES = ("peer", "group")
STEPS = 6
FACTS = 8
SMALL = pl.CostEstimate(flops=1, bytes_accessed=1, transcendentals=0)
ANY = pl.BlockSpec(memory_space=pl.ANY)
VMEM = pl.BlockSpec(memory_space=pltpu.VMEM)
SMEM = pl.BlockSpec(memory_space=pltpu.SMEM)


def swap(block, axis, mask):
    count = lax.axis_size(axis)
    return lax.ppermute(block, axis, [(i, i ^ mask) for i in range(count)])


def trade(block, peer_mask, member_mask):
    members = lax.axis_size("group")
    route = []
    for p in range(lax.axis_size("peer")):
        for g in range(members):
            other = (p ^ peer_mask) * members + (g ^ member_mask)
            route.append((p * members + g, other))
    return lax.ppermute(block, AXES, route)


def project(view_descriptors, embedding_matrix):
    raw = jnp.dot(view_descriptors, embedding_matrix, preferred_element_type=jnp.float32)
    row_length = jnp.sqrt(jnp.sum(raw * raw, axis=1, keepdims=True) + 1e-06)
    return (raw / row_length, row_length)


def after(value, *others):
    return lax.optimization_barrier((value, *others))[0]


def load(features, matrix, features_v, matrix_v, sems, begin, rows):
    depth = matrix_v.shape[0] // STEPS
    copies = [pltpu.make_async_copy(features.at[pl.ds(begin, rows)], features_v, sems.at[STEPS])]
    for k in range(STEPS):
        at = pl.ds(k * depth, depth)
        copies.append(pltpu.make_async_copy(matrix.at[at], matrix_v.at[at], sems.at[k]))
    for copy in copies:
        copy.start()
    return copies


def multiply(copies, features_v, matrix_v, raw):
    depth = matrix_v.shape[0] // STEPS
    copies[0].wait()
    for k in range(STEPS):
        at = slice(k * depth, (k + 1) * depth)
        copies[1 + k].wait()
        part = jnp.dot(features_v[:, at], matrix_v[at], preferred_element_type=jnp.float32)
        raw[...] = part if k == 0 else raw[...] + part
    return jnp.sqrt(jnp.sum(raw[...] * raw[...], axis=1, keepdims=True) + 1e-06)


def part_unit_kernel(ids, filled, features, matrix, unit, features_v, matrix_v, raw, sems):
    rows, width = raw.shape
    me = lax.axis_index("group")
    copies = load(features, matrix, features_v, matrix_v, sems, me * rows, rows)
    all_ids = ids[...].reshape(1, 4 * rows)
    here = all_ids[:, :rows]
    for k in range(1, 4):
        here = jnp.where(me == k, all_ids[:, k * rows : (k + 1) * rows], here)
    here = jnp.concatenate([here, jnp.zeros((1, 128 - rows), jnp.int32)], axis=1)
    count = jnp.full((1, 128), filled[0], jnp.int32)
    digits = [here & 255, here >> 8, count & 255, count >> 8]
    digits.append(jnp.zeros((1, width - 512), jnp.int32))
    facts = jnp.concatenate(digits, axis=1).astype(jnp.float32)
    row = lax.broadcasted_iota(jnp.int32, (FACTS, width), 0)
    facts = jnp.where(row == 0, facts, 0.0)
    length = multiply(copies, features_v, matrix_v, raw)
    unit[...] = jnp.concatenate([raw[...] / length, facts], axis=0).astype(jnp.bfloat16)


def part_unit(ids, filled, features, matrix):
    rows, depth = features.shape
    width = matrix.shape[1]
    part = rows // 4
    return pl.pallas_call(
        part_unit_kernel,
        out_shape=jax.ShapeDtypeStruct((part + FACTS, width), jnp.bfloat16),
        in_specs=[VMEM, SMEM, ANY, ANY],
        out_specs=VMEM,
        scratch_shapes=[
            pltpu.VMEM((part, depth), jnp.bfloat16),
            pltpu.VMEM((depth, width), jnp.bfloat16),
            pltpu.VMEM((part, width), jnp.float32),
            pltpu.SemaphoreType.DMA((STEPS + 1,)),
        ],
        compiler_params=pltpu.CompilerParams(vmem_limit_bytes=60 << 20),
        cost_estimate=pl.CostEstimate(
            flops=rows * depth * width, bytes_accessed=2 * depth * width, transcendentals=0
        ),
        name="part_unit",
    )(ids, filled, features, matrix)


def whole_unit_kernel(ids, features, matrix, unit, unit_bf, length, column, features_v, matrix_v, sems):
    rows = unit.shape[0]
    copies = load(features, matrix, features_v, matrix_v, sems, 0, rows)
    column[...] = jnp.broadcast_to(ids[...].reshape(1, rows).astype(jnp.float32), (128, rows)).T
    norm = multiply(copies, features_v, matrix_v, unit)
    length[...] = jnp.broadcast_to(norm, length.shape)
    unit[...] = unit[...] / norm
    unit_bf[...] = unit[...].astype(jnp.bfloat16)


def whole_unit(ids, features, matrix):
    rows, depth = features.shape
    width = matrix.shape[1]
    return pl.pallas_call(
        whole_unit_kernel,
        out_shape=[
            jax.ShapeDtypeStruct((rows, width), jnp.float32),
            jax.ShapeDtypeStruct((rows, width), jnp.bfloat16),
            jax.ShapeDtypeStruct((rows, 128), jnp.float32),
            jax.ShapeDtypeStruct((rows, 128), jnp.float32),
        ],
        in_specs=[VMEM, ANY, ANY],
        out_specs=[VMEM] * 4,
        scratch_shapes=[
            pltpu.VMEM((rows, depth), jnp.bfloat16),
            pltpu.VMEM((depth, width), jnp.bfloat16),
            pltpu.SemaphoreType.DMA((STEPS + 1,)),
        ],
        compiler_params=pltpu.CompilerParams(vmem_limit_bytes=28 << 20),
        cost_estimate=pl.CostEstimate(flops=2 * rows * depth * width, bytes_accessed=4 * depth * width, transcendentals=0),
        name="whole_unit",
    )(ids, features, matrix)


def pair_kernel(cuts, first, final, *refs):
    refs = list(refs)
    scale, shift, filled_here = refs[0][0], refs[1][0], refs[2][0]
    masks = [ref[0] for ref in refs[3:7]]
    ids_here, unit_bf = refs[7:9]
    del refs[:9]
    blocks = [refs.pop(0) for _ in cuts]
    if not first:
        old_dunit, old_losses = refs.pop(0), refs.pop(0)
    if final:
        unit, length = refs.pop(0), refs.pop(0)
        keep, send, stacked, total = refs
    else:
        total, losses_out, stacked = refs
    me = lax.axis_index("group")
    rows = unit_bf.shape[0]
    part = rows // 4
    offset = 0
    values = [block[...] for block in blocks]
    for value, (_, _, count, _) in zip(values, cuts):
        stacked[offset : offset + count] = value[:count]
        offset += count
    scores = lax.dot_general(
        unit_bf[...], stacked[...], (((1,), (1,)), ((), ())), preferred_element_type=jnp.float32
    )
    row = lax.broadcasted_iota(jnp.int32, (rows, 1), 0)
    used_here = row < filled_here
    lane = lax.broadcasted_iota(jnp.int32, (1, 128), 1)
    losses = jnp.zeros((1, 128), jnp.float32) if first else old_losses[0:1]
    slopes = []
    offset = 0
    for mask, begin, count, owner in cuts:
        turn = jnp.int32(-1)
        for e, other in enumerate(masks):
            turn = jnp.where(other == mask, jnp.bitwise_xor(me, e), turn)
        fact = values[owner][-FACTS:].astype(jnp.float32)[0:1]
        ids = fact[:, begin : begin + count] + 256.0 * fact[:, 128 + begin : 128 + begin + count]
        filled = fact[:, 256 : 256 + count] + 256.0 * fact[:, 384 : 384 + count]
        place = me * part + begin + lax.broadcasted_iota(jnp.int32, (1, count), 1)
        there = (place < filled.astype(jnp.int32)) & (turn >= 0)
        used = used_here & there
        signs = jnp.where(ids_here[:, :1] == ids, -1.0, 1.0)
        logits = signs * (scale * scores[:, offset : offset + count] + shift)
        small = jnp.exp(-jnp.abs(logits))
        penalty = jnp.maximum(logits, 0.0) + jnp.log1p(small)
        loss = jnp.sum(jnp.where(used, penalty, 0.0))
        losses = losses + jnp.where(lane == turn, loss, 0.0)
        gate = jnp.where(logits >= 0, 1.0, small) / (1.0 + small)
        slopes.append(jnp.where(used, signs * gate * scale, 0.0).astype(jnp.bfloat16))
        offset += count
    slopes = slopes[0] if len(slopes) == 1 else jnp.concatenate(slopes, axis=1)
    width = stacked.shape[1]
    step = width // 4
    for k in range(4):
        at = slice(k * step, (k + 1) * step)
        part = jnp.dot(slopes, stacked[:, at], preferred_element_type=jnp.float32)
        total[:, at] = part if first else old_dunit[:, at] + part
    if not final:
        losses_out[...] = jnp.broadcast_to(losses, losses_out.shape)
        return
    along = jnp.sum(unit[...] * total[...], axis=1, keepdims=True)
    total[...] = (total[...] - unit[...] * along) / length[:, :1]
    for k, other in enumerate((0, 2)):
        at = pl.ds(pl.multiple_of(jnp.bitwise_xor(me, other) * step, 128), step)
        keep[:rows, k * step : (k + 1) * step] = total[:, at]
        at = pl.ds(pl.multiple_of(jnp.bitwise_xor(me, other + 1) * step, 128), step)
        send[:rows, k * step : (k + 1) * step] = total[:, at]
    keep[rows:, :] = jnp.zeros((8, 2 * step), jnp.float32)
    keep[rows : rows + 1, 0:128] = losses
    send[rows:, :] = jnp.zeros((8, 2 * step), jnp.float32)
    send[rows : rows + 1, 0:128] = losses


def pair_terms(scalars, ids_here, unit_bf, blocks, cuts, old=None, final=None):
    rows, width = unit_bf.shape
    total = sum(count for _, _, count, _ in cuts)
    args = [*scalars, ids_here, unit_bf, *blocks]
    scratch = [pltpu.VMEM((total, width), jnp.bfloat16)]
    if old is not None:
        args += old
    if final is not None:
        args += final
        shapes = [jax.ShapeDtypeStruct((rows + 8, width // 2), jnp.float32)] * 2
        scratch += [pltpu.VMEM((rows, width), jnp.float32)]
    else:
        shapes = [
            jax.ShapeDtypeStruct((rows, width), jnp.float32),
            jax.ShapeDtypeStruct((8, 128), jnp.float32),
        ]
    return pl.pallas_call(
        functools.partial(pair_kernel, cuts, old is None, final is not None),
        out_shape=shapes,
        in_specs=[SMEM] * len(scalars) + [VMEM] * (len(args) - len(scalars)),
        out_specs=[VMEM] * len(shapes),
        scratch_shapes=scratch,
        compiler_params=pltpu.CompilerParams(vmem_limit_bytes=28 << 20),
        cost_estimate=pl.CostEstimate(flops=4 * rows * width * total, bytes_accessed=8 * rows * width, transcendentals=3 * rows * total),
        name="pair_terms",
    )(*args)


def combine_kernel(keep, arrived, own, send):
    rows, step = own.shape[0] - 8, own.shape[1]
    own[...] = keep[:, :step] + arrived[:, :step]
    send[:rows] = (keep[:rows, step:] + arrived[:rows, step:]).astype(jnp.bfloat16)
    losses = keep[rows : rows + 1, 0:128] + arrived[rows : rows + 1, 0:128]
    high = losses.astype(jnp.bfloat16).astype(jnp.float32)
    middle = (losses - high).astype(jnp.bfloat16).astype(jnp.float32)
    low = losses - high - middle
    line = lax.broadcasted_iota(jnp.int32, (16, 128), 0)
    packed = jnp.where(line == 0, high, jnp.where(line == 1, middle, jnp.where(line == 2, low, 0.0)))
    send[rows:] = jnp.zeros((16, step), jnp.bfloat16)
    send[rows:, 0:128] = packed.astype(jnp.bfloat16)


def combine(keep, arrived):
    rows, width = keep.shape[0] - 8, keep.shape[1]
    return pl.pallas_call(
        combine_kernel,
        out_shape=[
            jax.ShapeDtypeStruct((rows + 8, width // 2), jnp.float32),
            jax.ShapeDtypeStruct((rows + 16, width // 2), jnp.bfloat16),
        ],
        in_specs=[VMEM] * 2,
        out_specs=[VMEM] * 2,
        compiler_params=pltpu.CompilerParams(vmem_limit_bytes=16 << 20),
        cost_estimate=pl.CostEstimate(flops=rows * width, bytes_accessed=8 * rows * width, transcendentals=0),
        name="combine",
    )(keep, arrived)


def gradient_kernel(me, own, arrived, features, grad, loss, draw):
    rows = features.shape[1]

    @pl.when(pl.program_id(0) == 0)
    def _():
        draw[...] = (own[:rows] + arrived[:rows].astype(jnp.float32)).astype(jnp.bfloat16)
        parts = arrived[rows:, 0:128].astype(jnp.float32)
        total = own[rows : rows + 1, 0:128] + jnp.sum(parts, axis=0, keepdims=True)
        lane = lax.broadcasted_iota(jnp.int32, (1, 128), 1)
        value = jnp.sum(jnp.where(lane == me[0], total, 0.0))
        loss[0, 0] = value / (rows * rows)

    grad[...] = jnp.dot(features[...], draw[...], preferred_element_type=jnp.float32)


def gradient(me, own, arrived, features_t):
    depth, rows = features_t.shape
    width = own.shape[1]
    steps = 4
    return pl.pallas_call(
        gradient_kernel,
        out_shape=[
            jax.ShapeDtypeStruct((depth, width), jnp.float32),
            jax.ShapeDtypeStruct((1, 1), jnp.float32),
        ],
        grid=(steps,),
        in_specs=[
            SMEM,
            pl.BlockSpec(own.shape, lambda i: (0, 0)),
            pl.BlockSpec(arrived.shape, lambda i: (0, 0)),
            pl.BlockSpec((depth // steps, rows), lambda i: (i, 0)),
        ],
        out_specs=[pl.BlockSpec((depth // steps, width), lambda i: (i, 0)), SMEM],
        scratch_shapes=[pltpu.VMEM((rows, width), jnp.bfloat16)],
        compiler_params=pltpu.CompilerParams(vmem_limit_bytes=16 << 20),
        cost_estimate=pl.CostEstimate(flops=2 * rows * depth * width, bytes_accessed=4 * depth * width, transcendentals=0),
        name="gradient",
    )(me, own, arrived, features_t)


def small_plan(features, matrix, ids, filled, mask, scale, shift):
    rows = features.shape[0]
    part = rows // 4

    mine = part_unit(ids, filled, features, matrix)
    far = trade(mine, 6, 0)
    near = trade(mine, 1, 0)
    side = trade(mine, 2, 0)
    unit, unit_bf, length, column = whole_unit(ids, after(features, mine), matrix)
    others = [swap(after(mask, unit_bf), "group", k) for k in (1, 2, 3)]
    far_s = trade(after(far, unit_bf, *others), 2, 0)
    far_x = trade(after(far, unit_bf, *others), 1, 0)
    side_x = trade(after(side, unit_bf, near), 1, 0)
    common = ([scale, shift, filled, mask, *others], column, unit_bf)
    early = pair_terms(
        *common, [near, side, far], ((1, 0, part, 0), (2, 0, part, 1), (6, 0, part, 2))
    )
    last = trade(after(far_x, early[1]), 2, 0)
    middle = pair_terms(
        *common, [far_s, far_x], ((4, 0, part, 0), (7, 0, part, 1)), old=early
    )
    keep, send = pair_terms(
        *common,
        [side_x, last],
        ((3, 0, part, 0), (5, 0, part, 1)),
        old=middle,
        final=[unit, length],
    )
    own, send = combine(keep, swap(send, "group", 1))
    me = lax.axis_index("group")
    return gradient(me.reshape(1), own, swap(send, "group", 2), features.T)


def scatter_sum(block):
    count = lax.axis_size("group")
    me = lax.axis_index("group")
    rows, columns = block.shape
    block = block.reshape(rows, count, columns // count)
    kept = count
    for bit in range(count.bit_length() - 1):
        mine = jnp.bitwise_and(jnp.right_shift(me, bit), 1)
        pairs = block.reshape(rows, kept // 2, 2, -1)
        keep = lax.dynamic_index_in_dim(pairs, mine, 2, keepdims=False)
        send = lax.dynamic_index_in_dim(pairs, 1 - mine, 2, keepdims=False)
        if bit > 0:
            send = send.astype(jnp.bfloat16)
        block = keep + swap(send, "group", 1 << bit).astype(jnp.float32)
        kept //= 2
    return block.reshape(rows, columns // count)


def large_plan(features, matrix, ids, filled, mask, scale, shift):
    rows = features.shape[0]
    unit, length = project(features, matrix)
    unit_bf = unit.astype(jnp.bfloat16)
    current = (unit_bf, ids, filled)
    for bit in range(lax.axis_size("peer").bit_length() - 1):
        arrived = [swap(value, "peer", 1 << bit) for value in current]
        chosen = jnp.bitwise_and(jnp.right_shift(mask[0], bit), 1) == 1
        current = [jnp.where(chosen, new, old) for new, old in zip(arrived, current)]
    theirs, their_ids, their_filled = current
    scores = lax.dot_general(
        unit_bf, theirs, (((1,), (1,)), ((), ())), preferred_element_type=jnp.float32
    )
    index = jnp.arange(rows, dtype=jnp.int32)
    used = (index < filled[0])[:, None] & (index < their_filled[0])[None]
    signs = jnp.where(ids[:, None] == their_ids[None], 1.0, -1.0).astype(jnp.float32)
    logits = scale[0] * scores + shift[0]
    loss = jnp.sum(jnp.where(used, jax.nn.softplus(-signs * logits), 0.0))
    slopes = jnp.where(used, -signs * jax.nn.sigmoid(-signs * logits) * scale[0], 0.0)
    dunit = jnp.dot(slopes.astype(jnp.bfloat16), theirs, preferred_element_type=jnp.float32)
    tangent = (dunit - unit * jnp.sum(unit * dunit, axis=1, keepdims=True)) / length
    draw = scatter_sum(tangent).astype(jnp.bfloat16)
    grad = lax.dot_general(
        features, draw, (((0,), (0,)), ((), ())), preferred_element_type=jnp.float32
    )
    return (grad, (loss / (rows * rows)).reshape(1, 1))


def on_device(
    view_descriptors,
    embedding_matrix,
    picture_of_view,
    filled_view_places,
    companion_masks,
    score_scale,
    score_shift,
):
    small = lax.axis_size("peer") == 8 and lax.axis_size("group") == 4
    plan = small_plan if small else large_plan
    return plan(
        view_descriptors,
        embedding_matrix,
        picture_of_view,
        filled_view_places,
        companion_masks,
        score_scale,
        score_shift,
    )


def solution(mesh):
    placed = (P("peer", None), P(), P("peer"), P("peer"), P("group"), P(), P())
    return jax.shard_map(
        on_device,
        mesh=mesh,
        in_specs=placed,
        out_specs=(P("peer", "group"), P("peer", "group")),
        check_vma=False,
    )
```

```python
import functools

import jax
import jax.numpy as jnp
from jax import lax
from jax.experimental import pallas as pl
from jax.experimental.pallas import tpu as pltpu
from jax.sharding import PartitionSpec as P

AXES = ("peer", "group")
STEPS = 6
FACTS = 8
SMALL = pl.CostEstimate(flops=1, bytes_accessed=1, transcendentals=0)
ANY = pl.BlockSpec(memory_space=pl.ANY)
VMEM = pl.BlockSpec(memory_space=pltpu.VMEM)


def swap(block, axis, mask):
    count = lax.axis_size(axis)
    return lax.ppermute(block, axis, [(i, i ^ mask) for i in range(count)])


def trade(block, peer_mask, member_mask):
    members = lax.axis_size("group")
    route = []
    for p in range(lax.axis_size("peer")):
        for g in range(members):
            other = (p ^ peer_mask) * members + (g ^ member_mask)
            route.append((p * members + g, other))
    return lax.ppermute(block, AXES, route)


def project(view_descriptors, embedding_matrix):
    raw = jnp.dot(view_descriptors, embedding_matrix, preferred_element_type=jnp.float32)
    row_length = jnp.sqrt(jnp.sum(raw * raw, axis=1, keepdims=True) + 1e-06)
    return (raw / row_length, row_length)


def after(value, *others):
    return lax.optimization_barrier((value, *others))[0]


def load(features, matrix, features_v, matrix_v, sems, begin, rows):
    depth = matrix_v.shape[0] // STEPS
    copies = [pltpu.make_async_copy(features.at[pl.ds(begin, rows)], features_v, sems.at[STEPS])]
    for k in range(STEPS):
        at = pl.ds(k * depth, depth)
        copies.append(pltpu.make_async_copy(matrix.at[at], matrix_v.at[at], sems.at[k]))
    for copy in copies:
        copy.start()
    return copies


def multiply(copies, features_v, matrix_v, raw):
    depth = matrix_v.shape[0] // STEPS
    copies[0].wait()
    for k in range(STEPS):
        at = slice(k * depth, (k + 1) * depth)
        copies[1 + k].wait()
        part = jnp.dot(features_v[:, at], matrix_v[at], preferred_element_type=jnp.float32)
        raw[...] = part if k == 0 else raw[...] + part
    return jnp.sqrt(jnp.sum(raw[...] * raw[...], axis=1, keepdims=True) + 1e-06)


def part_unit_kernel(ids, filled, features, matrix, unit, ids_v, filled_s, features_v, matrix_v, raw, sems, small_sems):
    rows, width = raw.shape
    me = lax.axis_index("group")
    copies = load(features, matrix, features_v, matrix_v, sems, me * rows, rows)
    small = [
        pltpu.make_async_copy(ids, ids_v, small_sems.at[0]),
        pltpu.make_async_copy(filled, filled_s, small_sems.at[1]),
    ]
    for copy in small:
        copy.start()
    for copy in small:
        copy.wait()
    all_ids = ids_v[...].reshape(1, 4 * rows)
    here = all_ids[:, :rows]
    for k in range(1, 4):
        here = jnp.where(me == k, all_ids[:, k * rows : (k + 1) * rows], here)
    here = jnp.concatenate([here, jnp.zeros((1, 128 - rows), jnp.int32)], axis=1)
    count = jnp.full((1, 128), filled_s[0], jnp.int32)
    digits = [here & 255, here >> 8, count & 255, count >> 8]
    digits.append(jnp.zeros((1, width - 512), jnp.int32))
    facts = jnp.concatenate(digits, axis=1).astype(jnp.float32)
    row = lax.broadcasted_iota(jnp.int32, (FACTS, width), 0)
    facts = jnp.where(row == 0, facts, 0.0)
    length = multiply(copies, features_v, matrix_v, raw)
    unit[...] = jnp.concatenate([raw[...] / length, facts], axis=0).astype(jnp.bfloat16)


def part_unit(ids, filled, features, matrix):
    rows, depth = features.shape
    width = matrix.shape[1]
    part = rows // 4
    return pl.pallas_call(
        part_unit_kernel,
        out_shape=jax.ShapeDtypeStruct((part + FACTS, width), jnp.bfloat16),
        in_specs=[ANY] * 4,
        out_specs=VMEM,
        scratch_shapes=[
            pltpu.VMEM((rows,), jnp.int32),
            pltpu.SMEM((1,), jnp.int32),
            pltpu.VMEM((part, depth), jnp.bfloat16),
            pltpu.VMEM((depth, width), jnp.bfloat16),
            pltpu.VMEM((part, width), jnp.float32),
            pltpu.SemaphoreType.DMA((STEPS + 1,)),
            pltpu.SemaphoreType.DMA((2,)),
        ],
        compiler_params=pltpu.CompilerParams(vmem_limit_bytes=60 << 20),
        cost_estimate=pl.CostEstimate(
            flops=rows * depth * width, bytes_accessed=2 * depth * width, transcendentals=0
        ),
        name="part_unit",
    )(ids, filled, features, matrix)


def whole_unit_kernel(ids, filled, scale, shift, features, matrix, unit, unit_bf, length, column, numbers, features_v, matrix_v, sems):
    rows = unit.shape[0]
    copies = load(features, matrix, features_v, matrix_v, sems, 0, rows)
    column[...] = jnp.broadcast_to(ids[...].reshape(1, rows).astype(jnp.float32), (128, rows)).T
    numbers[0:1] = jnp.broadcast_to(scale[...].reshape(1, 1), (1, 128))
    numbers[1:2] = jnp.broadcast_to(shift[...].reshape(1, 1), (1, 128))
    numbers[2:3] = jnp.broadcast_to(filled[...].reshape(1, 1), (1, 128)).astype(jnp.float32)
    numbers[3:] = jnp.zeros((5, 128), jnp.float32)
    norm = multiply(copies, features_v, matrix_v, unit)
    length[...] = jnp.broadcast_to(norm, length.shape)
    unit[...] = unit[...] / norm
    unit_bf[...] = unit[...].astype(jnp.bfloat16)


def whole_unit(ids, filled, scale, shift, features, matrix):
    rows, depth = features.shape
    width = matrix.shape[1]
    return pl.pallas_call(
        whole_unit_kernel,
        out_shape=[
            jax.ShapeDtypeStruct((rows, width), jnp.float32),
            jax.ShapeDtypeStruct((rows, width), jnp.bfloat16),
            jax.ShapeDtypeStruct((rows, 128), jnp.float32),
            jax.ShapeDtypeStruct((rows, 128), jnp.float32),
            jax.ShapeDtypeStruct((8, 128), jnp.float32),
        ],
        in_specs=[VMEM] * 4 + [ANY] * 2,
        out_specs=[VMEM] * 5,
        scratch_shapes=[
            pltpu.VMEM((rows, depth), jnp.bfloat16),
            pltpu.VMEM((depth, width), jnp.bfloat16),
            pltpu.SemaphoreType.DMA((STEPS + 1,)),
        ],
        compiler_params=pltpu.CompilerParams(vmem_limit_bytes=28 << 20),
        cost_estimate=pl.CostEstimate(
            flops=2 * rows * depth * width, bytes_accessed=4 * depth * width, transcendentals=0
        ),
        name="whole_unit",
    )(ids, filled, scale, shift, features, matrix)


def pair_kernel(cuts, first, final, *refs):
    refs = list(refs)
    numbers = refs[0]
    masks = [ref[0:1] for ref in refs[1:5]]
    ids_here, unit_bf = refs[5:7]
    del refs[:7]
    blocks = [refs.pop(0) for _ in cuts]
    if not first:
        old_dunit, old_losses = refs.pop(0), refs.pop(0)
    if final:
        unit, length = refs.pop(0), refs.pop(0)
        keep, send, stacked, total = refs
    else:
        total, losses_out, stacked = refs
    me = lax.axis_index("group")
    rows = unit_bf.shape[0]
    part = rows // 4
    offset = 0
    values = [block[...] for block in blocks]
    for value, (_, _, count, _) in zip(values, cuts):
        stacked[offset : offset + count] = value[:count]
        offset += count
    scores = lax.dot_general(
        unit_bf[...], stacked[...], (((1,), (1,)), ((), ())), preferred_element_type=jnp.float32
    )
    row = lax.broadcasted_iota(jnp.int32, (rows, 1), 0)
    used_here = row < numbers[2:3, 0:1].astype(jnp.int32)
    lane = lax.broadcasted_iota(jnp.int32, (1, 128), 1)
    losses = jnp.zeros((1, 128), jnp.float32) if first else old_losses[0:1]
    slopes = []
    offset = 0
    for mask, begin, count, owner in cuts:
        turn = jnp.full((1, 128), -1, jnp.int32)
        for e, other in enumerate(masks):
            turn = jnp.where(other == mask, jnp.bitwise_xor(me, e), turn)
        fact = values[owner][-FACTS:].astype(jnp.float32)[0:1]
        ids = fact[:, begin : begin + count] + 256.0 * fact[:, 128 + begin : 128 + begin + count]
        filled = fact[:, 256 : 256 + count] + 256.0 * fact[:, 384 : 384 + count]
        place = me * part + begin + lax.broadcasted_iota(jnp.int32, (1, count), 1)
        there = (place < filled.astype(jnp.int32)) & (turn[:, :count] >= 0)
        used = used_here & there
        signs = jnp.where(ids_here[:, :1] == ids, -1.0, 1.0)
        scale, shift = numbers[0:1, :count], numbers[1:2, :count]
        logits = signs * (scale * scores[:, offset : offset + count] + shift)
        small = jnp.exp(-jnp.abs(logits))
        penalty = jnp.maximum(logits, 0.0) + jnp.log1p(small)
        loss = jnp.sum(jnp.where(used, penalty, 0.0))
        losses = losses + jnp.where(lane == turn, loss, 0.0)
        gate = jnp.where(logits >= 0, 1.0, small) / (1.0 + small)
        slopes.append(jnp.where(used, signs * gate * scale, 0.0).astype(jnp.bfloat16))
        offset += count
    slopes = slopes[0] if len(slopes) == 1 else jnp.concatenate(slopes, axis=1)
    width = stacked.shape[1]
    step = width // 4
    for k in range(4):
        at = slice(k * step, (k + 1) * step)
        part = jnp.dot(slopes, stacked[:, at], preferred_element_type=jnp.float32)
        total[:, at] = part if first else old_dunit[:, at] + part
    if not final:
        losses_out[...] = jnp.broadcast_to(losses, losses_out.shape)
        return
    along = jnp.sum(unit[...] * total[...], axis=1, keepdims=True)
    total[...] = (total[...] - unit[...] * along) / length[:, :1]
    for k, other in enumerate((0, 2)):
        at = pl.ds(pl.multiple_of(jnp.bitwise_xor(me, other) * step, 128), step)
        keep[:rows, k * step : (k + 1) * step] = total[:, at]
        at = pl.ds(pl.multiple_of(jnp.bitwise_xor(me, other + 1) * step, 128), step)
        send[:rows, k * step : (k + 1) * step] = total[:, at]
    keep[rows:, :] = jnp.zeros((8, 2 * step), jnp.float32)
    keep[rows : rows + 1, 0:128] = losses
    send[rows:, :] = jnp.zeros((8, 2 * step), jnp.float32)
    send[rows : rows + 1, 0:128] = losses


def pair_terms(numbers, masks, ids_here, unit_bf, blocks, cuts, old=None, final=None):
    rows, width = unit_bf.shape
    total = sum(count for _, _, count, _ in cuts)
    args = [numbers, *masks, ids_here, unit_bf, *blocks]
    scratch = [pltpu.VMEM((total, width), jnp.bfloat16)]
    if old is not None:
        args += old
    if final is not None:
        args += final
        shapes = [jax.ShapeDtypeStruct((rows + 8, width // 2), jnp.float32)] * 2
        scratch += [pltpu.VMEM((rows, width), jnp.float32)]
    else:
        shapes = [
            jax.ShapeDtypeStruct((rows, width), jnp.float32),
            jax.ShapeDtypeStruct((8, 128), jnp.float32),
        ]
    return pl.pallas_call(
        functools.partial(pair_kernel, cuts, old is None, final is not None),
        out_shape=shapes,
        in_specs=[VMEM] * len(args),
        out_specs=[VMEM] * len(shapes),
        scratch_shapes=scratch,
        compiler_params=pltpu.CompilerParams(vmem_limit_bytes=28 << 20),
        cost_estimate=pl.CostEstimate(flops=4 * rows * width * total, bytes_accessed=8 * rows * width, transcendentals=3 * rows * total),
        name="pair_terms",
    )(*args)


def combine_kernel(keep, arrived, own, send):
    rows, step = own.shape[0] - 8, own.shape[1]
    own[...] = keep[:, :step] + arrived[:, :step]
    send[:rows] = (keep[:rows, step:] + arrived[:rows, step:]).astype(jnp.bfloat16)
    losses = keep[rows : rows + 1, 0:128] + arrived[rows : rows + 1, 0:128]
    high = losses.astype(jnp.bfloat16).astype(jnp.float32)
    middle = (losses - high).astype(jnp.bfloat16).astype(jnp.float32)
    low = losses - high - middle
    line = lax.broadcasted_iota(jnp.int32, (16, 128), 0)
    packed = jnp.where(line == 0, high, jnp.where(line == 1, middle, jnp.where(line == 2, low, 0.0)))
    send[rows:] = jnp.zeros((16, step), jnp.bfloat16)
    send[rows:, 0:128] = packed.astype(jnp.bfloat16)


def combine(keep, arrived):
    rows, width = keep.shape[0] - 8, keep.shape[1]
    return pl.pallas_call(
        combine_kernel,
        out_shape=[
            jax.ShapeDtypeStruct((rows + 8, width // 2), jnp.float32),
            jax.ShapeDtypeStruct((rows + 16, width // 2), jnp.bfloat16),
        ],
        in_specs=[VMEM] * 2,
        out_specs=[VMEM] * 2,
        compiler_params=pltpu.CompilerParams(vmem_limit_bytes=16 << 20),
        cost_estimate=pl.CostEstimate(flops=rows * width, bytes_accessed=8 * rows * width, transcendentals=0),
        name="combine",
    )(keep, arrived)


def gradient_kernel(own, arrived, features, grad, loss, draw, parts, sems):
    rows = features.shape[1]
    steps, height = parts.shape[:2]
    draw[...] = (own[:rows] + arrived[:rows].astype(jnp.float32)).astype(jnp.bfloat16)
    copies = []
    for k in range(steps):
        at = pl.ds(k * height, height)
        parts[k] = jnp.dot(features[at], draw[...], preferred_element_type=jnp.float32)
        copies.append(pltpu.make_async_copy(parts.at[k], grad.at[at], sems.at[k]))
        copies[k].start()
    low = jnp.sum(arrived[rows:, 0:128].astype(jnp.float32), axis=0, keepdims=True)
    total = own[rows : rows + 1, 0:128] + low
    lane = lax.broadcasted_iota(jnp.int32, (1, 128), 1)
    mine = jnp.where(lane == lax.axis_index("group"), total, 0.0)
    loss[...] = jnp.sum(mine, axis=1, keepdims=True) / (rows * rows)
    for copy in copies:
        copy.wait()


def gradient(own, arrived, features_t):
    depth, rows = features_t.shape
    width = own.shape[1]
    steps = 6
    return pl.pallas_call(
        gradient_kernel,
        out_shape=[
            jax.ShapeDtypeStruct((depth, width), jnp.float32),
            jax.ShapeDtypeStruct((1, 1), jnp.float32),
        ],
        in_specs=[VMEM] * 3,
        out_specs=[ANY, VMEM],
        scratch_shapes=[
            pltpu.VMEM((rows, width), jnp.bfloat16),
            pltpu.VMEM((steps, depth // steps, width), jnp.float32),
            pltpu.SemaphoreType.DMA((steps,)),
        ],
        compiler_params=pltpu.CompilerParams(vmem_limit_bytes=16 << 20),
        cost_estimate=pl.CostEstimate(
            flops=2 * rows * depth * width, bytes_accessed=4 * depth * width, transcendentals=0
        ),
        name="gradient",
    )(own, arrived, features_t)


def small_plan(features, matrix, ids, filled, mask, scale, shift):
    rows = features.shape[0]
    part = rows // 4

    mine = part_unit(ids, filled, features, matrix)
    mask = jnp.broadcast_to(after(mask, mine)[:, None], (8, 128))
    far = trade(mine, 6, 0)
    near = trade(mine, 1, 0)
    side = trade(mine, 2, 0)
    unit, unit_bf, length, column, numbers = whole_unit(
        ids, filled, scale, shift, after(features, mine), matrix
    )
    others = [swap(mask, "group", k) for k in (1, 2, 3)]
    far_s = trade(after(far, unit_bf, *others), 2, 0)
    far_x = trade(after(far, unit_bf, *others), 1, 0)
    side_x = trade(after(side, unit_bf, near), 1, 0)
    common = (numbers, [mask, *others], column, unit_bf)
    early = pair_terms(
        *common, [near, side, far], ((1, 0, part, 0), (2, 0, part, 1), (6, 0, part, 2))
    )
    last = trade(after(far_x, early[1]), 2, 0)
    middle = pair_terms(
        *common, [far_s, far_x], ((4, 0, part, 0), (7, 0, part, 1)), old=early
    )
    keep, send = pair_terms(
        *common,
        [side_x, last],
        ((3, 0, part, 0), (5, 0, part, 1)),
        old=middle,
        final=[unit, length],
    )
    own, send = combine(keep, swap(send, "group", 1))
    return gradient(own, swap(send, "group", 2), features.T)


def scatter_sum(block):
    count = lax.axis_size("group")
    me = lax.axis_index("group")
    rows, columns = block.shape
    block = block.reshape(rows, count, columns // count)
    kept = count
    for bit in range(count.bit_length() - 1):
        mine = jnp.bitwise_and(jnp.right_shift(me, bit), 1)
        pairs = block.reshape(rows, kept // 2, 2, -1)
        keep = lax.dynamic_index_in_dim(pairs, mine, 2, keepdims=False)
        send = lax.dynamic_index_in_dim(pairs, 1 - mine, 2, keepdims=False)
        if bit > 0:
            send = send.astype(jnp.bfloat16)
        block = keep + swap(send, "group", 1 << bit).astype(jnp.float32)
        kept //= 2
    return block.reshape(rows, columns // count)


def large_plan(features, matrix, ids, filled, mask, scale, shift):
    rows = features.shape[0]
    unit, length = project(features, matrix)
    unit_bf = unit.astype(jnp.bfloat16)
    current = (unit_bf, ids, filled)
    for bit in range(lax.axis_size("peer").bit_length() - 1):
        arrived = [swap(value, "peer", 1 << bit) for value in current]
        chosen = jnp.bitwise_and(jnp.right_shift(mask[0], bit), 1) == 1
        current = [jnp.where(chosen, new, old) for new, old in zip(arrived, current)]
    theirs, their_ids, their_filled = current
    scores = lax.dot_general(
        unit_bf, theirs, (((1,), (1,)), ((), ())), preferred_element_type=jnp.float32
    )
    index = jnp.arange(rows, dtype=jnp.int32)
    used = (index < filled[0])[:, None] & (index < their_filled[0])[None]
    signs = jnp.where(ids[:, None] == their_ids[None], 1.0, -1.0).astype(jnp.float32)
    logits = scale[0] * scores + shift[0]
    loss = jnp.sum(jnp.where(used, jax.nn.softplus(-signs * logits), 0.0))
    slopes = jnp.where(used, -signs * jax.nn.sigmoid(-signs * logits) * scale[0], 0.0)
    dunit = jnp.dot(slopes.astype(jnp.bfloat16), theirs, preferred_element_type=jnp.float32)
    tangent = (dunit - unit * jnp.sum(unit * dunit, axis=1, keepdims=True)) / length
    draw = scatter_sum(tangent).astype(jnp.bfloat16)
    grad = lax.dot_general(
        features, draw, (((0,), (0,)), ((), ())), preferred_element_type=jnp.float32
    )
    return (grad, (loss / (rows * rows)).reshape(1, 1))


def on_device(
    view_descriptors,
    embedding_matrix,
    picture_of_view,
    filled_view_places,
    companion_masks,
    score_scale,
    score_shift,
):
    small = lax.axis_size("peer") == 8 and lax.axis_size("group") == 4
    plan = small_plan if small else large_plan
    return plan(
        view_descriptors,
        embedding_matrix,
        picture_of_view,
        filled_view_places,
        companion_masks,
        score_scale,
        score_shift,
    )


def solution(mesh):
    placed = (P("peer", None), P(), P("peer"), P("peer"), P("group"), P(), P())
    return jax.shard_map(
        on_device,
        mesh=mesh,
        in_specs=placed,
        out_specs=(P("peer", "group"), P("peer", "group")),
        check_vma=False,
    )
```

```python
import functools

import jax
import jax.numpy as jnp
from jax import lax
from jax.experimental import pallas as pl
from jax.experimental.pallas import tpu as pltpu
from jax.sharding import PartitionSpec as P

AXES = ("peer", "group")
STEPS = 3
FACTS = 8
SMALL = pl.CostEstimate(flops=1, bytes_accessed=1, transcendentals=0)
ANY = pl.BlockSpec(memory_space=pl.ANY)
VMEM = pl.BlockSpec(memory_space=pltpu.VMEM)


def swap(block, axis, mask):
    count = lax.axis_size(axis)
    return lax.ppermute(block, axis, [(i, i ^ mask) for i in range(count)])


def trade(block, peer_mask, member_mask):
    members = lax.axis_size("group")
    route = []
    for p in range(lax.axis_size("peer")):
        for g in range(members):
            other = (p ^ peer_mask) * members + (g ^ member_mask)
            route.append((p * members + g, other))
    return lax.ppermute(block, AXES, route)


def project(view_descriptors, embedding_matrix):
    raw = jnp.dot(view_descriptors, embedding_matrix, preferred_element_type=jnp.float32)
    row_length = jnp.sqrt(jnp.sum(raw * raw, axis=1, keepdims=True) + 1e-06)
    return (raw / row_length, row_length)


def after(value, *others):
    return lax.optimization_barrier((value, *others))[0]


def load(features, matrix, features_v, matrix_v, sems, begin, rows):
    depth = matrix_v.shape[0] // STEPS
    copies = [pltpu.make_async_copy(features.at[pl.ds(begin, rows)], features_v, sems.at[STEPS])]
    for k in range(STEPS):
        at = pl.ds(k * depth, depth)
        copies.append(pltpu.make_async_copy(matrix.at[at], matrix_v.at[at], sems.at[k]))
    for copy in copies:
        copy.start()
    return copies


def multiply(copies, features_v, matrix_v, raw):
    depth = matrix_v.shape[0] // STEPS
    copies[0].wait()
    for k in range(STEPS):
        at = slice(k * depth, (k + 1) * depth)
        copies[1 + k].wait()
        part = jnp.dot(features_v[:, at], matrix_v[at], preferred_element_type=jnp.float32)
        raw[...] = part if k == 0 else raw[...] + part
    return jnp.sqrt(jnp.sum(raw[...] * raw[...], axis=1, keepdims=True) + 1e-06)


def part_unit_kernel(ids, filled, features, matrix, unit, ids_v, filled_s, features_v, matrix_v, raw, sems, small_sems):
    rows, width = raw.shape
    me = lax.axis_index("group")
    copies = load(features, matrix, features_v, matrix_v, sems, me * rows, rows)
    small = [
        pltpu.make_async_copy(ids, ids_v, small_sems.at[0]),
        pltpu.make_async_copy(filled, filled_s, small_sems.at[1]),
    ]
    for copy in small:
        copy.start()
    for copy in small:
        copy.wait()
    all_ids = ids_v[...].reshape(1, 4 * rows)
    here = all_ids[:, :rows]
    for k in range(1, 4):
        here = jnp.where(me == k, all_ids[:, k * rows : (k + 1) * rows], here)
    here = jnp.concatenate([here, jnp.zeros((1, 128 - rows), jnp.int32)], axis=1)
    count = jnp.full((1, 128), filled_s[0], jnp.int32)
    digits = [here & 255, here >> 8, count & 255, count >> 8]
    digits.append(jnp.zeros((1, width - 512), jnp.int32))
    facts = jnp.concatenate(digits, axis=1).astype(jnp.float32)
    row = lax.broadcasted_iota(jnp.int32, (FACTS, width), 0)
    facts = jnp.where(row == 0, facts, 0.0)
    length = multiply(copies, features_v, matrix_v, raw)
    unit[...] = jnp.concatenate([raw[...] / length, facts], axis=0).astype(jnp.bfloat16)


def part_unit(ids, filled, features, matrix):
    rows, depth = features.shape
    width = matrix.shape[1]
    part = rows // 4
    return pl.pallas_call(
        part_unit_kernel,
        out_shape=jax.ShapeDtypeStruct((part + FACTS, width), jnp.bfloat16),
        in_specs=[ANY] * 4,
        out_specs=VMEM,
        scratch_shapes=[
            pltpu.VMEM((rows,), jnp.int32),
            pltpu.SMEM((1,), jnp.int32),
            pltpu.VMEM((part, depth), jnp.bfloat16),
            pltpu.VMEM((depth, width), jnp.bfloat16),
            pltpu.VMEM((part, width), jnp.float32),
            pltpu.SemaphoreType.DMA((STEPS + 1,)),
            pltpu.SemaphoreType.DMA((2,)),
        ],
        compiler_params=pltpu.CompilerParams(vmem_limit_bytes=60 << 20),
        cost_estimate=pl.CostEstimate(
            flops=rows * depth * width, bytes_accessed=2 * depth * width, transcendentals=0
        ),
        name="part_unit",
    )(ids, filled, features, matrix)


def whole_unit_kernel(ids, filled, scale, shift, features, matrix, unit, unit_bf, length, column, numbers, features_v, matrix_v, sems):
    rows = unit.shape[0]
    copies = load(features, matrix, features_v, matrix_v, sems, 0, rows)
    column[...] = jnp.broadcast_to(ids[...].reshape(1, rows).astype(jnp.float32), (128, rows)).T
    numbers[0:1] = jnp.broadcast_to(scale[...].reshape(1, 1), (1, 128))
    numbers[1:2] = jnp.broadcast_to(shift[...].reshape(1, 1), (1, 128))
    numbers[2:3] = jnp.broadcast_to(filled[...].reshape(1, 1), (1, 128)).astype(jnp.float32)
    numbers[3:] = jnp.zeros((5, 128), jnp.float32)
    norm = multiply(copies, features_v, matrix_v, unit)
    length[...] = jnp.broadcast_to(norm, length.shape)
    unit[...] = unit[...] / norm
    unit_bf[...] = unit[...].astype(jnp.bfloat16)


def whole_unit(ids, filled, scale, shift, features, matrix):
    rows, depth = features.shape
    width = matrix.shape[1]
    return pl.pallas_call(
        whole_unit_kernel,
        out_shape=[
            jax.ShapeDtypeStruct((rows, width), jnp.float32),
            jax.ShapeDtypeStruct((rows, width), jnp.bfloat16),
            jax.ShapeDtypeStruct((rows, 128), jnp.float32),
            jax.ShapeDtypeStruct((rows, 128), jnp.float32),
            jax.ShapeDtypeStruct((8, 128), jnp.float32),
        ],
        in_specs=[VMEM] * 4 + [ANY] * 2,
        out_specs=[VMEM] * 5,
        scratch_shapes=[
            pltpu.VMEM((rows, depth), jnp.bfloat16),
            pltpu.VMEM((depth, width), jnp.bfloat16),
            pltpu.SemaphoreType.DMA((STEPS + 1,)),
        ],
        compiler_params=pltpu.CompilerParams(vmem_limit_bytes=28 << 20),
        cost_estimate=pl.CostEstimate(
            flops=2 * rows * depth * width, bytes_accessed=4 * depth * width, transcendentals=0
        ),
        name="whole_unit",
    )(ids, filled, scale, shift, features, matrix)


def pair_kernel(cuts, first, final, window, *refs):
    refs = list(refs)
    numbers = refs[0]
    masks = [ref[0:1] for ref in refs[1:5]]
    ids_here, unit_bf = refs[5:7]
    del refs[:7]
    blocks = [refs.pop(0) for _ in cuts]
    if not first:
        old_dunit, old_losses = refs.pop(0), refs.pop(0)
    if final:
        unit, length = refs.pop(0), refs.pop(0)
        keep, send, stacked, total = refs
    else:
        total, losses_out, stacked = refs
    me = lax.axis_index("group")
    here = slice(*window)
    rows = window[1] - window[0]
    part = unit_bf.shape[0] // 4
    offset = 0
    values = [block[...] for block in blocks]
    for value, (_, _, count, _) in zip(values, cuts):
        stacked[offset : offset + count] = value[:count]
        offset += count
    scores = lax.dot_general(
        unit_bf[here], stacked[...], (((1,), (1,)), ((), ())), preferred_element_type=jnp.float32
    )
    row = window[0] + lax.broadcasted_iota(jnp.int32, (rows, 1), 0)
    used_here = row < numbers[2:3, 0:1].astype(jnp.int32)
    lane = lax.broadcasted_iota(jnp.int32, (1, 128), 1)
    losses = jnp.zeros((1, 128), jnp.float32) if first or window[0] else old_losses[0:1]
    slopes = []
    offset = 0
    for mask, begin, count, owner in cuts:
        turn = jnp.full((1, 128), -1, jnp.int32)
        for e, other in enumerate(masks):
            turn = jnp.where(other == mask, jnp.bitwise_xor(me, e), turn)
        fact = values[owner][-FACTS:].astype(jnp.float32)[0:1]
        ids = fact[:, begin : begin + count] + 256.0 * fact[:, 128 + begin : 128 + begin + count]
        filled = fact[:, 256 : 256 + count] + 256.0 * fact[:, 384 : 384 + count]
        place = me * part + begin + lax.broadcasted_iota(jnp.int32, (1, count), 1)
        there = (place < filled.astype(jnp.int32)) & (turn[:, :count] >= 0)
        used = used_here & there
        signs = jnp.where(ids_here[here, :1] == ids, -1.0, 1.0)
        scale, shift = numbers[0:1, :count], numbers[1:2, :count]
        logits = signs * (scale * scores[:, offset : offset + count] + shift)
        small = jnp.exp(-jnp.abs(logits))
        penalty = jnp.maximum(logits, 0.0) + jnp.log1p(small)
        loss = jnp.sum(jnp.where(used, penalty, 0.0))
        losses = losses + jnp.where(lane == turn, loss, 0.0)
        gate = jnp.where(logits >= 0, 1.0, small) / (1.0 + small)
        slopes.append(jnp.where(used, signs * gate * scale, 0.0).astype(jnp.bfloat16))
        offset += count
    slopes = slopes[0] if len(slopes) == 1 else jnp.concatenate(slopes, axis=1)
    width = stacked.shape[1]
    step = width // 4
    for k in range(4):
        at = slice(k * step, (k + 1) * step)
        part = jnp.dot(slopes, stacked[:, at], preferred_element_type=jnp.float32)
        total[:, at] = part if first else old_dunit[here, at] + part
    if not final:
        losses_out[...] = jnp.broadcast_to(losses, losses_out.shape)
        return
    along = jnp.sum(unit[here] * total[...], axis=1, keepdims=True)
    total[...] = (total[...] - unit[here] * along) / length[here, :1]
    for k, other in enumerate((0, 2)):
        at = pl.ds(pl.multiple_of(jnp.bitwise_xor(me, other) * step, 128), step)
        keep[:rows, k * step : (k + 1) * step] = total[:, at]
        at = pl.ds(pl.multiple_of(jnp.bitwise_xor(me, other + 1) * step, 128), step)
        send[:rows, k * step : (k + 1) * step] = total[:, at]
    keep[rows:, :] = jnp.zeros((8, 2 * step), jnp.float32)
    keep[rows : rows + 1, 0:128] = losses
    send[rows:, :] = jnp.zeros((8, 2 * step), jnp.float32)
    send[rows : rows + 1, 0:128] = losses


def pair_terms(numbers, masks, ids_here, unit_bf, blocks, cuts, old=None, final=None, window=None):
    window = window or (0, unit_bf.shape[0])
    rows, width = window[1] - window[0], unit_bf.shape[1]
    total = sum(count for _, _, count, _ in cuts)
    args = [numbers, *masks, ids_here, unit_bf, *blocks]
    scratch = [pltpu.VMEM((total, width), jnp.bfloat16)]
    if old is not None:
        args += old
    if final is not None:
        args += final
        shapes = [jax.ShapeDtypeStruct((rows + 8, width // 2), jnp.float32)] * 2
        scratch += [pltpu.VMEM((rows, width), jnp.float32)]
    else:
        shapes = [
            jax.ShapeDtypeStruct((rows, width), jnp.float32),
            jax.ShapeDtypeStruct((8, 128), jnp.float32),
        ]
    return pl.pallas_call(
        functools.partial(pair_kernel, cuts, old is None, final is not None, window),
        out_shape=shapes,
        in_specs=[VMEM] * len(args),
        out_specs=[VMEM] * len(shapes),
        scratch_shapes=scratch,
        compiler_params=pltpu.CompilerParams(vmem_limit_bytes=28 << 20),
        cost_estimate=pl.CostEstimate(flops=4 * rows * width * total, bytes_accessed=8 * rows * width, transcendentals=3 * rows * total),
        name="pair_terms",
    )(*args)


def combine_kernel(keep, arrived, own, send):
    rows, step = own.shape[0] - 8, own.shape[1]
    own[...] = keep[:, :step] + arrived[:, :step]
    send[:rows] = (keep[:rows, step:] + arrived[:rows, step:]).astype(jnp.bfloat16)
    losses = keep[rows : rows + 1, 0:128] + arrived[rows : rows + 1, 0:128]
    high = losses.astype(jnp.bfloat16).astype(jnp.float32)
    middle = (losses - high).astype(jnp.bfloat16).astype(jnp.float32)
    low = losses - high - middle
    line = lax.broadcasted_iota(jnp.int32, (16, 128), 0)
    packed = jnp.where(line == 0, high, jnp.where(line == 1, middle, jnp.where(line == 2, low, 0.0)))
    send[rows:] = jnp.zeros((16, step), jnp.bfloat16)
    send[rows:, 0:128] = packed.astype(jnp.bfloat16)


def combine(keep, arrived):
    rows, width = keep.shape[0] - 8, keep.shape[1]
    return pl.pallas_call(
        combine_kernel,
        out_shape=[
            jax.ShapeDtypeStruct((rows + 8, width // 2), jnp.float32),
            jax.ShapeDtypeStruct((rows + 16, width // 2), jnp.bfloat16),
        ],
        in_specs=[VMEM] * 2,
        out_specs=[VMEM] * 2,
        compiler_params=pltpu.CompilerParams(vmem_limit_bytes=16 << 20),
        cost_estimate=pl.CostEstimate(flops=rows * width, bytes_accessed=8 * rows * width, transcendentals=0),
        name="combine",
    )(keep, arrived)


def gradient_kernel(own_a, own_b, arrived_a, arrived_b, features, grad, loss, draw, parts, sems):
    rows = features.shape[1]
    half = rows // 2
    steps, height = parts.shape[:2]
    draw[:half] = (own_a[:half] + arrived_a[:half].astype(jnp.float32)).astype(jnp.bfloat16)
    draw[half:] = (own_b[:half] + arrived_b[:half].astype(jnp.float32)).astype(jnp.bfloat16)
    copies = []
    for k in range(steps):
        at = pl.ds(k * height, height)
        parts[k] = jnp.dot(features[at], draw[...], preferred_element_type=jnp.float32)
        copies.append(pltpu.make_async_copy(parts.at[k], grad.at[at], sems.at[k]))
        copies[k].start()
    total = own_a[half : half + 1, 0:128] + own_b[half : half + 1, 0:128]
    for arrived in (arrived_a, arrived_b):
        total += jnp.sum(arrived[half:, 0:128].astype(jnp.float32), axis=0, keepdims=True)
    lane = lax.broadcasted_iota(jnp.int32, (1, 128), 1)
    mine = jnp.where(lane == lax.axis_index("group"), total, 0.0)
    loss[...] = jnp.sum(mine, axis=1, keepdims=True) / (rows * rows)
    for copy in copies:
        copy.wait()


def gradient(own, arrived, features_t):
    depth, rows = features_t.shape
    width = own[0].shape[1]
    steps = 6
    return pl.pallas_call(
        gradient_kernel,
        out_shape=[
            jax.ShapeDtypeStruct((depth, width), jnp.float32),
            jax.ShapeDtypeStruct((1, 1), jnp.float32),
        ],
        in_specs=[VMEM] * 5,
        out_specs=[ANY, VMEM],
        scratch_shapes=[
            pltpu.VMEM((rows, width), jnp.bfloat16),
            pltpu.VMEM((steps, depth // steps, width), jnp.float32),
            pltpu.SemaphoreType.DMA((steps,)),
        ],
        compiler_params=pltpu.CompilerParams(vmem_limit_bytes=16 << 20),
        cost_estimate=pl.CostEstimate(
            flops=2 * rows * depth * width, bytes_accessed=4 * depth * width, transcendentals=0
        ),
        name="gradient",
    )(*own, *arrived, features_t)


def small_plan(features, matrix, ids, filled, mask, scale, shift):
    rows = features.shape[0]
    part = rows // 4

    mine = part_unit(ids, filled, features, matrix)
    mask = jnp.broadcast_to(after(mask, mine)[:, None], (8, 128))
    far = trade(mine, 6, 0)
    near = trade(mine, 1, 0)
    side = trade(mine, 2, 0)
    unit, unit_bf, length, column, numbers = whole_unit(
        ids, filled, scale, shift, after(features, mine), matrix
    )
    others = [swap(mask, "group", k) for k in (1, 2, 3)]
    far_s = trade(after(far, unit_bf, *others), 2, 0)
    far_x = trade(after(far, unit_bf, *others), 1, 0)
    side_x = trade(after(side, unit_bf, near), 1, 0)
    common = (numbers, [mask, *others], column, unit_bf)
    early = pair_terms(
        *common, [near, side, far], ((1, 0, part, 0), (2, 0, part, 1), (6, 0, part, 2))
    )
    last = trade(after(far_x, early[1]), 2, 0)
    middle = pair_terms(
        *common, [far_s, far_x], ((4, 0, part, 0), (7, 0, part, 1)), old=early
    )
    own, arrived = [], []
    sent = []
    for window in ((0, rows // 2), (rows // 2, rows)):
        keep, send = pair_terms(
            *common,
            [side_x, last],
            ((3, 0, part, 0), (5, 0, part, 1)),
            old=middle,
            final=[unit, length],
            window=window,
        )
        sent.append((keep, swap(send, "group", 1)))
    for keep, received in sent:
        kept, send = combine(keep, received)
        own.append(kept)
        arrived.append(swap(send, "group", 2))
    return gradient(own, arrived, features.T)


def scatter_sum(block):
    count = lax.axis_size("group")
    me = lax.axis_index("group")
    rows, columns = block.shape
    block = block.reshape(rows, count, columns // count)
    kept = count
    for bit in range(count.bit_length() - 1):
        mine = jnp.bitwise_and(jnp.right_shift(me, bit), 1)
        pairs = block.reshape(rows, kept // 2, 2, -1)
        keep = lax.dynamic_index_in_dim(pairs, mine, 2, keepdims=False)
        send = lax.dynamic_index_in_dim(pairs, 1 - mine, 2, keepdims=False)
        if bit > 0:
            send = send.astype(jnp.bfloat16)
        block = keep + swap(send, "group", 1 << bit).astype(jnp.float32)
        kept //= 2
    return block.reshape(rows, columns // count)


def large_plan(features, matrix, ids, filled, mask, scale, shift):
    rows = features.shape[0]
    unit, length = project(features, matrix)
    unit_bf = unit.astype(jnp.bfloat16)
    current = (unit_bf, ids, filled)
    for bit in range(lax.axis_size("peer").bit_length() - 1):
        arrived = [swap(value, "peer", 1 << bit) for value in current]
        chosen = jnp.bitwise_and(jnp.right_shift(mask[0], bit), 1) == 1
        current = [jnp.where(chosen, new, old) for new, old in zip(arrived, current)]
    theirs, their_ids, their_filled = current
    scores = lax.dot_general(
        unit_bf, theirs, (((1,), (1,)), ((), ())), preferred_element_type=jnp.float32
    )
    index = jnp.arange(rows, dtype=jnp.int32)
    used = (index < filled[0])[:, None] & (index < their_filled[0])[None]
    signs = jnp.where(ids[:, None] == their_ids[None], 1.0, -1.0).astype(jnp.float32)
    logits = scale[0] * scores + shift[0]
    loss = jnp.sum(jnp.where(used, jax.nn.softplus(-signs * logits), 0.0))
    slopes = jnp.where(used, -signs * jax.nn.sigmoid(-signs * logits) * scale[0], 0.0)
    dunit = jnp.dot(slopes.astype(jnp.bfloat16), theirs, preferred_element_type=jnp.float32)
    tangent = (dunit - unit * jnp.sum(unit * dunit, axis=1, keepdims=True)) / length
    draw = scatter_sum(tangent).astype(jnp.bfloat16)
    grad = lax.dot_general(
        features, draw, (((0,), (0,)), ((), ())), preferred_element_type=jnp.float32
    )
    return (grad, (loss / (rows * rows)).reshape(1, 1))


def on_device(
    view_descriptors,
    embedding_matrix,
    picture_of_view,
    filled_view_places,
    companion_masks,
    score_scale,
    score_shift,
):
    small = lax.axis_size("peer") == 8 and lax.axis_size("group") == 4
    plan = small_plan if small else large_plan
    return plan(
        view_descriptors,
        embedding_matrix,
        picture_of_view,
        filled_view_places,
        companion_masks,
        score_scale,
        score_shift,
    )


def solution(mesh):
    placed = (P("peer", None), P(), P("peer"), P("peer"), P("group"), P(), P())
    return jax.shard_map(
        on_device,
        mesh=mesh,
        in_specs=placed,
        out_specs=(P("peer", "group"), P("peer", "group")),
        check_vma=False,
    )
```

```python
import functools

import jax
import jax.numpy as jnp
from jax import lax
from jax.experimental import pallas as pl
from jax.experimental.pallas import tpu as pltpu
from jax.sharding import PartitionSpec as P

AXES = ("peer", "group")
STEPS = 3
FACTS = 16
LANES = 128
SMALL = pl.CostEstimate(flops=1, bytes_accessed=1, transcendentals=0)
ANY = pl.BlockSpec(memory_space=pl.ANY)
VMEM = pl.BlockSpec(memory_space=pltpu.VMEM)


def swap(block, axis, mask):
    count = lax.axis_size(axis)
    return lax.ppermute(block, axis, [(i, i ^ mask) for i in range(count)])


def trade(block, peer_mask, member_mask):
    members = lax.axis_size("group")
    route = []
    for p in range(lax.axis_size("peer")):
        for g in range(members):
            other = (p ^ peer_mask) * members + (g ^ member_mask)
            route.append((p * members + g, other))
    return lax.ppermute(block, AXES, route)


def project(view_descriptors, embedding_matrix):
    raw = jnp.dot(view_descriptors, embedding_matrix, preferred_element_type=jnp.float32)
    row_length = jnp.sqrt(jnp.sum(raw * raw, axis=1, keepdims=True) + 1e-06)
    return (raw / row_length, row_length)


def after(value, *others):
    return lax.optimization_barrier((value, *others))[0]


def load(features, matrix, features_v, matrix_v, sems, begin, rows):
    depth = matrix_v.shape[0] // STEPS
    copies = [pltpu.make_async_copy(features.at[pl.ds(begin, rows)], features_v, sems.at[STEPS])]
    for k in range(STEPS):
        at = pl.ds(k * depth, depth)
        copies.append(pltpu.make_async_copy(matrix.at[at], matrix_v.at[at], sems.at[k]))
    for copy in copies:
        copy.start()
    return copies


def multiply(copies, features_v, matrix_v, raw):
    depth = matrix_v.shape[0] // STEPS
    copies[0].wait()
    for k in range(STEPS):
        at = slice(k * depth, (k + 1) * depth)
        copies[1 + k].wait()
        part = jnp.dot(features_v[:, at], matrix_v[at], preferred_element_type=jnp.float32)
        raw[...] = part if k == 0 else raw[...] + part
    return jnp.sqrt(jnp.sum(raw[...] * raw[...], axis=1, keepdims=True) + 1e-06)


def part_unit_kernel(ids, filled, features, matrix, unit, ids_v, filled_s, features_v, matrix_v, raw, sems, small_sems):
    rows, width = raw.shape
    me = lax.axis_index("group")
    copies = load(features, matrix, features_v, matrix_v, sems, me * rows, rows)
    small = [
        pltpu.make_async_copy(ids, ids_v, small_sems.at[0]),
        pltpu.make_async_copy(filled, filled_s, small_sems.at[1]),
    ]
    for copy in small:
        copy.start()
    for copy in small:
        copy.wait()
    all_ids = ids_v[...].reshape(1, 4 * rows)
    here = all_ids[:, :rows]
    for k in range(1, 4):
        here = jnp.where(me == k, all_ids[:, k * rows : (k + 1) * rows], here)
    here = jnp.concatenate([here, jnp.zeros((1, LANES - rows), jnp.int32)], axis=1)
    count = jnp.full((1, LANES), filled_s[0], jnp.int32)
    row = lax.broadcasted_iota(jnp.int32, (FACTS, LANES), 0)
    facts = jnp.zeros((FACTS, LANES), jnp.int32)
    for k, digit in enumerate((here & 255, here >> 8, count & 255, count >> 8)):
        facts = jnp.where(row == k, digit, facts)
    length = multiply(copies, features_v, matrix_v, raw)
    chunks = width // LANES
    for k in range(chunks):
        value = raw[:, k * LANES : (k + 1) * LANES] / length
        unit[k * rows : (k + 1) * rows] = value.astype(jnp.bfloat16)
    unit[chunks * rows :] = facts.astype(jnp.float32).astype(jnp.bfloat16)


def part_unit(ids, filled, features, matrix):
    rows, depth = features.shape
    width = matrix.shape[1]
    part = rows // 4
    return pl.pallas_call(
        part_unit_kernel,
        out_shape=jax.ShapeDtypeStruct((part * width // LANES + FACTS, LANES), jnp.bfloat16),
        in_specs=[ANY] * 4,
        out_specs=VMEM,
        scratch_shapes=[
            pltpu.VMEM((rows,), jnp.int32),
            pltpu.SMEM((1,), jnp.int32),
            pltpu.VMEM((part, depth), jnp.bfloat16),
            pltpu.VMEM((depth, width), jnp.bfloat16),
            pltpu.VMEM((part, width), jnp.float32),
            pltpu.SemaphoreType.DMA((STEPS + 1,)),
            pltpu.SemaphoreType.DMA((2,)),
        ],
        compiler_params=pltpu.CompilerParams(vmem_limit_bytes=60 << 20),
        cost_estimate=pl.CostEstimate(
            flops=rows * depth * width, bytes_accessed=2 * depth * width, transcendentals=0
        ),
        name="part_unit",
    )(ids, filled, features, matrix)


def whole_unit_kernel(ids, filled, scale, shift, features, matrix, unit, unit_bf, length, column, numbers, features_v, matrix_v, sems):
    rows = unit.shape[0]
    copies = load(features, matrix, features_v, matrix_v, sems, 0, rows)
    column[...] = jnp.broadcast_to(ids[...].reshape(1, rows).astype(jnp.float32), (128, rows)).T
    numbers[0:1] = jnp.broadcast_to(scale[...].reshape(1, 1), (1, 128))
    numbers[1:2] = jnp.broadcast_to(shift[...].reshape(1, 1), (1, 128))
    numbers[2:3] = jnp.broadcast_to(filled[...].reshape(1, 1), (1, 128)).astype(jnp.float32)
    numbers[3:] = jnp.zeros((5, 128), jnp.float32)
    norm = multiply(copies, features_v, matrix_v, unit)
    length[...] = jnp.broadcast_to(norm, length.shape)
    unit[...] = unit[...] / norm
    unit_bf[...] = unit[...].astype(jnp.bfloat16)


def whole_unit(ids, filled, scale, shift, features, matrix):
    rows, depth = features.shape
    width = matrix.shape[1]
    return pl.pallas_call(
        whole_unit_kernel,
        out_shape=[
            jax.ShapeDtypeStruct((rows, width), jnp.float32),
            jax.ShapeDtypeStruct((rows, width), jnp.bfloat16),
            jax.ShapeDtypeStruct((rows, 128), jnp.float32),
            jax.ShapeDtypeStruct((rows, 128), jnp.float32),
            jax.ShapeDtypeStruct((8, 128), jnp.float32),
        ],
        in_specs=[VMEM] * 4 + [ANY] * 2,
        out_specs=[VMEM] * 5,
        scratch_shapes=[
            pltpu.VMEM((rows, depth), jnp.bfloat16),
            pltpu.VMEM((depth, width), jnp.bfloat16),
            pltpu.SemaphoreType.DMA((STEPS + 1,)),
        ],
        compiler_params=pltpu.CompilerParams(vmem_limit_bytes=28 << 20),
        cost_estimate=pl.CostEstimate(
            flops=2 * rows * depth * width, bytes_accessed=4 * depth * width, transcendentals=0
        ),
        name="whole_unit",
    )(ids, filled, scale, shift, features, matrix)


def pair_kernel(cuts, first, final, window, *refs):
    refs = list(refs)
    numbers = refs[0]
    masks = [ref[0:1] for ref in refs[1:5]]
    ids_here, unit_bf = refs[5:7]
    del refs[:7]
    blocks = [refs.pop(0) for _ in cuts]
    if not first:
        old_dunit, old_losses = refs.pop(0), refs.pop(0)
    if final:
        unit, length = refs.pop(0), refs.pop(0)
        keep, send, stacked, total = refs
    else:
        total, losses_out, stacked = refs
    me = lax.axis_index("group")
    here = slice(*window)
    rows = window[1] - window[0]
    part = unit_bf.shape[0] // 4
    offset = 0
    for block, (_, _, count, _) in zip(blocks, cuts):
        for k in range(stacked.shape[1] // LANES):
            at = slice(k * LANES, (k + 1) * LANES)
            stacked[offset : offset + count, at] = block[k * count : (k + 1) * count]
        offset += count
    scores = lax.dot_general(
        unit_bf[here], stacked[...], (((1,), (1,)), ((), ())), preferred_element_type=jnp.float32
    )
    row = window[0] + lax.broadcasted_iota(jnp.int32, (rows, 1), 0)
    used_here = row < numbers[2:3, 0:1].astype(jnp.int32)
    lane = lax.broadcasted_iota(jnp.int32, (1, 128), 1)
    losses = jnp.zeros((1, 128), jnp.float32) if first or window[0] else old_losses[0:1]
    slopes = []
    offset = 0
    for mask, begin, count, owner in cuts:
        turn = jnp.full((1, 128), -1, jnp.int32)
        for e, other in enumerate(masks):
            turn = jnp.where(other == mask, jnp.bitwise_xor(me, e), turn)
        last = blocks[owner].shape[0] - FACTS
        fact = blocks[owner][last:].astype(jnp.float32)
        ids = fact[0:1, begin : begin + count] + 256.0 * fact[1:2, begin : begin + count]
        filled = fact[2:3, :count] + 256.0 * fact[3:4, :count]
        place = me * part + begin + lax.broadcasted_iota(jnp.int32, (1, count), 1)
        there = (place < filled.astype(jnp.int32)) & (turn[:, :count] >= 0)
        used = used_here & there
        signs = jnp.where(ids_here[here, :1] == ids, -1.0, 1.0)
        scale, shift = numbers[0:1, :count], numbers[1:2, :count]
        logits = signs * (scale * scores[:, offset : offset + count] + shift)
        small = jnp.exp(-jnp.abs(logits))
        penalty = jnp.maximum(logits, 0.0) + jnp.log1p(small)
        loss = jnp.sum(jnp.where(used, penalty, 0.0))
        losses = losses + jnp.where(lane == turn, loss, 0.0)
        gate = jnp.where(logits >= 0, 1.0, small) / (1.0 + small)
        slopes.append(jnp.where(used, signs * gate * scale, 0.0).astype(jnp.bfloat16))
        offset += count
    slopes = slopes[0] if len(slopes) == 1 else jnp.concatenate(slopes, axis=1)
    width = stacked.shape[1]
    step = width // 4
    for k in range(4):
        at = slice(k * step, (k + 1) * step)
        part = jnp.dot(slopes, stacked[:, at], preferred_element_type=jnp.float32)
        total[:, at] = part if first else old_dunit[here, at] + part
    if not final:
        losses_out[...] = jnp.broadcast_to(losses, losses_out.shape)
        return
    along = jnp.sum(unit[here] * total[...], axis=1, keepdims=True)
    total[...] = (total[...] - unit[here] * along) / length[here, :1]
    for k, other in enumerate((0, 2)):
        at = pl.ds(pl.multiple_of(jnp.bitwise_xor(me, other) * step, 128), step)
        keep[:rows, k * step : (k + 1) * step] = total[:, at]
        at = pl.ds(pl.multiple_of(jnp.bitwise_xor(me, other + 1) * step, 128), step)
        send[:rows, k * step : (k + 1) * step] = total[:, at]
    keep[rows:, :] = jnp.zeros((8, 2 * step), jnp.float32)
    keep[rows : rows + 1, 0:128] = losses
    send[rows:, :] = jnp.zeros((8, 2 * step), jnp.float32)
    send[rows : rows + 1, 0:128] = losses


def pair_terms(numbers, masks, ids_here, unit_bf, blocks, cuts, old=None, final=None, window=None):
    window = window or (0, unit_bf.shape[0])
    rows, width = window[1] - window[0], unit_bf.shape[1]
    total = sum(count for _, _, count, _ in cuts)
    args = [numbers, *masks, ids_here, unit_bf, *blocks]
    scratch = [pltpu.VMEM((total, width), jnp.bfloat16)]
    if old is not None:
        args += old
    if final is not None:
        args += final
        shapes = [jax.ShapeDtypeStruct((rows + 8, width // 2), jnp.float32)] * 2
        scratch += [pltpu.VMEM((rows, width), jnp.float32)]
    else:
        shapes = [
            jax.ShapeDtypeStruct((rows, width), jnp.float32),
            jax.ShapeDtypeStruct((8, 128), jnp.float32),
        ]
    return pl.pallas_call(
        functools.partial(pair_kernel, cuts, old is None, final is not None, window),
        out_shape=shapes,
        in_specs=[VMEM] * len(args),
        out_specs=[VMEM] * len(shapes),
        scratch_shapes=scratch,
        compiler_params=pltpu.CompilerParams(vmem_limit_bytes=28 << 20),
        cost_estimate=pl.CostEstimate(flops=4 * rows * width * total, bytes_accessed=8 * rows * width, transcendentals=3 * rows * total),
        name="pair_terms",
    )(*args)


def combine_kernel(keep, arrived, own, send):
    rows, step = own.shape[0] - 8, own.shape[1]
    own[...] = keep[:, :step] + arrived[:, :step]
    send[:rows] = (keep[:rows, step:] + arrived[:rows, step:]).astype(jnp.bfloat16)
    losses = keep[rows : rows + 1, 0:128] + arrived[rows : rows + 1, 0:128]
    high = losses.astype(jnp.bfloat16).astype(jnp.float32)
    middle = (losses - high).astype(jnp.bfloat16).astype(jnp.float32)
    low = losses - high - middle
    line = lax.broadcasted_iota(jnp.int32, (16, 128), 0)
    packed = jnp.where(line == 0, high, jnp.where(line == 1, middle, jnp.where(line == 2, low, 0.0)))
    send[rows:] = jnp.zeros((16, step), jnp.bfloat16)
    send[rows:, 0:128] = packed.astype(jnp.bfloat16)


def combine(keep, arrived):
    rows, width = keep.shape[0] - 8, keep.shape[1]
    return pl.pallas_call(
        combine_kernel,
        out_shape=[
            jax.ShapeDtypeStruct((rows + 8, width // 2), jnp.float32),
            jax.ShapeDtypeStruct((rows + 16, width // 2), jnp.bfloat16),
        ],
        in_specs=[VMEM] * 2,
        out_specs=[VMEM] * 2,
        compiler_params=pltpu.CompilerParams(vmem_limit_bytes=16 << 20),
        cost_estimate=pl.CostEstimate(flops=rows * width, bytes_accessed=8 * rows * width, transcendentals=0),
        name="combine",
    )(keep, arrived)


def gradient_kernel(own_a, own_b, arrived_a, arrived_b, features, grad, loss, draw, parts, sems):
    rows = features.shape[1]
    half = rows // 2
    steps, height = parts.shape[:2]
    draw[:half] = (own_a[:half] + arrived_a[:half].astype(jnp.float32)).astype(jnp.bfloat16)
    draw[half:] = (own_b[:half] + arrived_b[:half].astype(jnp.float32)).astype(jnp.bfloat16)
    copies = []
    for k in range(steps):
        at = pl.ds(k * height, height)
        parts[k] = jnp.dot(features[at], draw[...], preferred_element_type=jnp.float32)
        copies.append(pltpu.make_async_copy(parts.at[k], grad.at[at], sems.at[k]))
        copies[k].start()
    total = own_a[half : half + 1, 0:128] + own_b[half : half + 1, 0:128]
    for arrived in (arrived_a, arrived_b):
        total += jnp.sum(arrived[half:, 0:128].astype(jnp.float32), axis=0, keepdims=True)
    lane = lax.broadcasted_iota(jnp.int32, (1, 128), 1)
    mine = jnp.where(lane == lax.axis_index("group"), total, 0.0)
    loss[...] = jnp.sum(mine, axis=1, keepdims=True) / (rows * rows)
    for copy in copies:
        copy.wait()


def gradient(own, arrived, features_t):
    depth, rows = features_t.shape
    width = own[0].shape[1]
    steps = 6
    return pl.pallas_call(
        gradient_kernel,
        out_shape=[
            jax.ShapeDtypeStruct((depth, width), jnp.float32),
            jax.ShapeDtypeStruct((1, 1), jnp.float32),
        ],
        in_specs=[VMEM] * 5,
        out_specs=[ANY, VMEM],
        scratch_shapes=[
            pltpu.VMEM((rows, width), jnp.bfloat16),
            pltpu.VMEM((steps, depth // steps, width), jnp.float32),
            pltpu.SemaphoreType.DMA((steps,)),
        ],
        compiler_params=pltpu.CompilerParams(vmem_limit_bytes=16 << 20),
        cost_estimate=pl.CostEstimate(
            flops=2 * rows * depth * width, bytes_accessed=4 * depth * width, transcendentals=0
        ),
        name="gradient",
    )(*own, *arrived, features_t)


def small_plan(features, matrix, ids, filled, mask, scale, shift):
    rows = features.shape[0]
    part = rows // 4

    mine = part_unit(ids, filled, features, matrix)
    mask = jnp.broadcast_to(after(mask, mine)[:, None], (8, 128))
    far = trade(mine, 6, 0)
    near = trade(mine, 1, 0)
    side = trade(mine, 2, 0)
    unit, unit_bf, length, column, numbers = whole_unit(
        ids, filled, scale, shift, after(features, mine), matrix
    )
    others = [swap(mask, "group", k) for k in (1, 2, 3)]
    far_s = trade(after(far, unit_bf, *others), 2, 0)
    far_x = trade(after(far, unit_bf, *others), 1, 0)
    side_x = trade(after(side, unit_bf, near), 1, 0)
    common = (numbers, [mask, *others], column, unit_bf)
    early = pair_terms(
        *common, [near, side, far], ((1, 0, part, 0), (2, 0, part, 1), (6, 0, part, 2))
    )
    last = trade(after(far_x, early[1]), 2, 0)
    middle = pair_terms(
        *common, [far_s, far_x], ((4, 0, part, 0), (7, 0, part, 1)), old=early
    )
    own, arrived = [], []
    sent = []
    for window in ((0, rows // 2), (rows // 2, rows)):
        keep, send = pair_terms(
            *common,
            [side_x, last],
            ((3, 0, part, 0), (5, 0, part, 1)),
            old=middle,
            final=[unit, length],
            window=window,
        )
        sent.append((keep, swap(send, "group", 1)))
    for keep, received in sent:
        kept, send = combine(keep, received)
        own.append(kept)
        arrived.append(swap(send, "group", 2))
    return gradient(own, arrived, features.T)


def scatter_sum(block):
    count = lax.axis_size("group")
    me = lax.axis_index("group")
    rows, columns = block.shape
    block = block.reshape(rows, count, columns // count)
    kept = count
    for bit in range(count.bit_length() - 1):
        mine = jnp.bitwise_and(jnp.right_shift(me, bit), 1)
        pairs = block.reshape(rows, kept // 2, 2, -1)
        keep = lax.dynamic_index_in_dim(pairs, mine, 2, keepdims=False)
        send = lax.dynamic_index_in_dim(pairs, 1 - mine, 2, keepdims=False)
        if bit > 0:
            send = send.astype(jnp.bfloat16)
        block = keep + swap(send, "group", 1 << bit).astype(jnp.float32)
        kept //= 2
    return block.reshape(rows, columns // count)


def large_plan(features, matrix, ids, filled, mask, scale, shift):
    rows = features.shape[0]
    unit, length = project(features, matrix)
    unit_bf = unit.astype(jnp.bfloat16)
    current = (unit_bf, ids, filled)
    for bit in range(lax.axis_size("peer").bit_length() - 1):
        arrived = [swap(value, "peer", 1 << bit) for value in current]
        chosen = jnp.bitwise_and(jnp.right_shift(mask[0], bit), 1) == 1
        current = [jnp.where(chosen, new, old) for new, old in zip(arrived, current)]
    theirs, their_ids, their_filled = current
    scores = lax.dot_general(
        unit_bf, theirs, (((1,), (1,)), ((), ())), preferred_element_type=jnp.float32
    )
    index = jnp.arange(rows, dtype=jnp.int32)
    used = (index < filled[0])[:, None] & (index < their_filled[0])[None]
    signs = jnp.where(ids[:, None] == their_ids[None], 1.0, -1.0).astype(jnp.float32)
    logits = scale[0] * scores + shift[0]
    loss = jnp.sum(jnp.where(used, jax.nn.softplus(-signs * logits), 0.0))
    slopes = jnp.where(used, -signs * jax.nn.sigmoid(-signs * logits) * scale[0], 0.0)
    dunit = jnp.dot(slopes.astype(jnp.bfloat16), theirs, preferred_element_type=jnp.float32)
    tangent = (dunit - unit * jnp.sum(unit * dunit, axis=1, keepdims=True)) / length
    draw = scatter_sum(tangent).astype(jnp.bfloat16)
    grad = lax.dot_general(
        features, draw, (((0,), (0,)), ((), ())), preferred_element_type=jnp.float32
    )
    return (grad, (loss / (rows * rows)).reshape(1, 1))


def on_device(
    view_descriptors,
    embedding_matrix,
    picture_of_view,
    filled_view_places,
    companion_masks,
    score_scale,
    score_shift,
):
    small = lax.axis_size("peer") == 8 and lax.axis_size("group") == 4
    plan = small_plan if small else large_plan
    return plan(
        view_descriptors,
        embedding_matrix,
        picture_of_view,
        filled_view_places,
        companion_masks,
        score_scale,
        score_shift,
    )


def solution(mesh):
    placed = (P("peer", None), P(), P("peer"), P("peer"), P("group"), P(), P())
    return jax.shard_map(
        on_device,
        mesh=mesh,
        in_specs=placed,
        out_specs=(P("peer", "group"), P("peer", "group")),
        check_vma=False,
    )
```

```python
import functools

import jax
import jax.numpy as jnp
from jax import lax
from jax.experimental import pallas as pl
from jax.experimental.pallas import tpu as pltpu
from jax.sharding import PartitionSpec as P

AXES = ("peer", "group")
STEPS = 3
FACTS = 16
LANES = 128
SMALL = pl.CostEstimate(flops=1, bytes_accessed=1, transcendentals=0)
ANY = pl.BlockSpec(memory_space=pl.ANY)
VMEM = pl.BlockSpec(memory_space=pltpu.VMEM)


def swap(block, axis, mask):
    count = lax.axis_size(axis)
    return lax.ppermute(block, axis, [(i, i ^ mask) for i in range(count)])


def trade(block, peer_mask, member_mask):
    members = lax.axis_size("group")
    route = []
    for p in range(lax.axis_size("peer")):
        for g in range(members):
            other = (p ^ peer_mask) * members + (g ^ member_mask)
            route.append((p * members + g, other))
    return lax.ppermute(block, AXES, route)


def project(view_descriptors, embedding_matrix):
    raw = jnp.dot(view_descriptors, embedding_matrix, preferred_element_type=jnp.float32)
    row_length = jnp.sqrt(jnp.sum(raw * raw, axis=1, keepdims=True) + 1e-06)
    return (raw / row_length, row_length)


def after(value, *others):
    return lax.optimization_barrier((value, *others))[0]


def load(features, matrix, features_v, matrix_v, sems, begin, rows):
    depth = matrix_v.shape[0] // STEPS
    copies = [pltpu.make_async_copy(features.at[pl.ds(begin, rows)], features_v, sems.at[STEPS])]
    for k in range(STEPS):
        at = pl.ds(k * depth, depth)
        copies.append(pltpu.make_async_copy(matrix.at[at], matrix_v.at[at], sems.at[k]))
    for copy in copies:
        copy.start()
    return copies


def multiply(copies, features_v, matrix_v, raw):
    depth = matrix_v.shape[0] // STEPS
    copies[0].wait()
    for k in range(STEPS):
        at = slice(k * depth, (k + 1) * depth)
        copies[1 + k].wait()
        part = jnp.dot(features_v[:, at], matrix_v[at], preferred_element_type=jnp.float32)
        raw[...] = part if k == 0 else raw[...] + part
    return jnp.sqrt(jnp.sum(raw[...] * raw[...], axis=1, keepdims=True) + 1e-06)


def part_unit_kernel(ids, filled, features, matrix, unit, ids_v, filled_s, features_v, matrix_v, raw, sems, small_sems):
    rows, width = raw.shape
    me = lax.axis_index("group")
    small = [
        pltpu.make_async_copy(ids, ids_v, small_sems.at[0]),
        pltpu.make_async_copy(filled, filled_s, small_sems.at[1]),
    ]
    for copy in small:
        copy.start()
    copies = load(features, matrix, features_v, matrix_v, sems, me * rows, rows)
    for copy in small:
        copy.wait()
    all_ids = ids_v[...].reshape(1, 4 * rows)
    here = all_ids[:, :rows]
    for k in range(1, 4):
        here = jnp.where(me == k, all_ids[:, k * rows : (k + 1) * rows], here)
    here = jnp.concatenate([here, jnp.zeros((1, LANES - rows), jnp.int32)], axis=1)
    count = jnp.full((1, LANES), filled_s[0], jnp.int32)
    row = lax.broadcasted_iota(jnp.int32, (FACTS, LANES), 0)
    facts = jnp.zeros((FACTS, LANES), jnp.int32)
    for k, digit in enumerate((here & 255, here >> 8, count & 255, count >> 8)):
        facts = jnp.where(row == k, digit, facts)
    length = multiply(copies, features_v, matrix_v, raw)
    chunks = width // LANES
    for k in range(chunks):
        value = raw[:, k * LANES : (k + 1) * LANES] / length
        unit[k * rows : (k + 1) * rows] = value.astype(jnp.bfloat16)
    unit[chunks * rows :] = facts.astype(jnp.float32).astype(jnp.bfloat16)


def part_unit(ids, filled, features, matrix):
    rows, depth = features.shape
    width = matrix.shape[1]
    part = rows // 4
    return pl.pallas_call(
        part_unit_kernel,
        out_shape=jax.ShapeDtypeStruct((part * width // LANES + FACTS, LANES), jnp.bfloat16),
        in_specs=[ANY] * 4,
        out_specs=VMEM,
        scratch_shapes=[
            pltpu.VMEM((rows,), jnp.int32),
            pltpu.SMEM((1,), jnp.int32),
            pltpu.VMEM((part, depth), jnp.bfloat16),
            pltpu.VMEM((depth, width), jnp.bfloat16),
            pltpu.VMEM((part, width), jnp.float32),
            pltpu.SemaphoreType.DMA((STEPS + 1,)),
            pltpu.SemaphoreType.DMA((2,)),
        ],
        compiler_params=pltpu.CompilerParams(vmem_limit_bytes=60 << 20),
        cost_estimate=pl.CostEstimate(
            flops=rows * depth * width, bytes_accessed=2 * depth * width, transcendentals=0
        ),
        name="part_unit",
    )(ids, filled, features, matrix)


def whole_unit_kernel(ids, filled, scale, shift, features, matrix, unit, unit_bf, length, column, numbers, features_v, matrix_v, sems):
    rows = unit.shape[0]
    copies = load(features, matrix, features_v, matrix_v, sems, 0, rows)
    column[...] = jnp.broadcast_to(ids[...].reshape(1, rows).astype(jnp.float32), (128, rows)).T
    numbers[0:1] = jnp.broadcast_to(scale[...].reshape(1, 1), (1, 128))
    numbers[1:2] = jnp.broadcast_to(shift[...].reshape(1, 1), (1, 128))
    numbers[2:3] = jnp.broadcast_to(filled[...].reshape(1, 1), (1, 128)).astype(jnp.float32)
    numbers[3:] = jnp.zeros((5, 128), jnp.float32)
    norm = multiply(copies, features_v, matrix_v, unit)
    length[...] = jnp.broadcast_to(norm, length.shape)
    unit[...] = unit[...] / norm
    unit_bf[...] = unit[...].astype(jnp.bfloat16)


def whole_unit(ids, filled, scale, shift, features, matrix):
    rows, depth = features.shape
    width = matrix.shape[1]
    return pl.pallas_call(
        whole_unit_kernel,
        out_shape=[
            jax.ShapeDtypeStruct((rows, width), jnp.float32),
            jax.ShapeDtypeStruct((rows, width), jnp.bfloat16),
            jax.ShapeDtypeStruct((rows, 128), jnp.float32),
            jax.ShapeDtypeStruct((rows, 128), jnp.float32),
            jax.ShapeDtypeStruct((8, 128), jnp.float32),
        ],
        in_specs=[VMEM] * 4 + [ANY] * 2,
        out_specs=[VMEM] * 5,
        scratch_shapes=[
            pltpu.VMEM((rows, depth), jnp.bfloat16),
            pltpu.VMEM((depth, width), jnp.bfloat16),
            pltpu.SemaphoreType.DMA((STEPS + 1,)),
        ],
        compiler_params=pltpu.CompilerParams(vmem_limit_bytes=28 << 20),
        cost_estimate=pl.CostEstimate(
            flops=2 * rows * depth * width, bytes_accessed=4 * depth * width, transcendentals=0
        ),
        name="whole_unit",
    )(ids, filled, scale, shift, features, matrix)


def pair_kernel(cuts, first, final, window, *refs):
    refs = list(refs)
    numbers = refs[0]
    masks = [ref[0:1] for ref in refs[1:5]]
    ids_here, unit_bf = refs[5:7]
    del refs[:7]
    blocks = [refs.pop(0) for _ in cuts]
    if not first:
        old_dunit, old_losses = refs.pop(0), refs.pop(0)
    if final:
        unit, length = refs.pop(0), refs.pop(0)
        keep, send, stacked, total = refs
    else:
        total, losses_out, stacked = refs
    me = lax.axis_index("group")
    here = slice(*window)
    rows = window[1] - window[0]
    part = unit_bf.shape[0] // 4
    offset = 0
    for block, (_, _, count, _) in zip(blocks, cuts):
        for k in range(stacked.shape[1] // LANES):
            at = slice(k * LANES, (k + 1) * LANES)
            stacked[offset : offset + count, at] = block[k * count : (k + 1) * count]
        offset += count
    scores = lax.dot_general(
        unit_bf[here], stacked[...], (((1,), (1,)), ((), ())), preferred_element_type=jnp.float32
    )
    row = window[0] + lax.broadcasted_iota(jnp.int32, (rows, 1), 0)
    used_here = row < numbers[2:3, 0:1].astype(jnp.int32)
    lane = lax.broadcasted_iota(jnp.int32, (1, 128), 1)
    losses = jnp.zeros((1, 128), jnp.float32) if first or window[0] else old_losses[0:1]
    slopes = []
    offset = 0
    for mask, begin, count, owner in cuts:
        turn = jnp.full((1, 128), -1, jnp.int32)
        for e, other in enumerate(masks):
            turn = jnp.where(other == mask, jnp.bitwise_xor(me, e), turn)
        last = blocks[owner].shape[0] - FACTS
        fact = blocks[owner][last:].astype(jnp.float32)
        ids = fact[0:1, begin : begin + count] + 256.0 * fact[1:2, begin : begin + count]
        filled = fact[2:3, :count] + 256.0 * fact[3:4, :count]
        place = me * part + begin + lax.broadcasted_iota(jnp.int32, (1, count), 1)
        there = (place < filled.astype(jnp.int32)) & (turn[:, :count] >= 0)
        used = used_here & there
        signs = jnp.where(ids_here[here, :1] == ids, -1.0, 1.0)
        scale, shift = numbers[0:1, :count], numbers[1:2, :count]
        logits = signs * (scale * scores[:, offset : offset + count] + shift)
        small = jnp.exp(-jnp.abs(logits))
        penalty = jnp.maximum(logits, 0.0) + jnp.log1p(small)
        loss = jnp.sum(jnp.where(used, penalty, 0.0))
        losses = losses + jnp.where(lane == turn, loss, 0.0)
        gate = jnp.where(logits >= 0, 1.0, small) / (1.0 + small)
        slopes.append(jnp.where(used, signs * gate * scale, 0.0).astype(jnp.bfloat16))
        offset += count
    slopes = slopes[0] if len(slopes) == 1 else jnp.concatenate(slopes, axis=1)
    width = stacked.shape[1]
    step = width // 4
    for k in range(4):
        at = slice(k * step, (k + 1) * step)
        part = jnp.dot(slopes, stacked[:, at], preferred_element_type=jnp.float32)
        total[:, at] = part if first else old_dunit[here, at] + part
    if not final:
        losses_out[...] = jnp.broadcast_to(losses, losses_out.shape)
        return
    along = jnp.sum(unit[here] * total[...], axis=1, keepdims=True)
    total[...] = (total[...] - unit[here] * along) / length[here, :1]
    for k, other in enumerate((0, 2)):
        at = pl.ds(pl.multiple_of(jnp.bitwise_xor(me, other) * step, 128), step)
        keep[:rows, k * step : (k + 1) * step] = total[:, at]
        at = pl.ds(pl.multiple_of(jnp.bitwise_xor(me, other + 1) * step, 128), step)
        send[:rows, k * step : (k + 1) * step] = total[:, at]
    keep[rows:, :] = jnp.zeros((8, 2 * step), jnp.float32)
    keep[rows : rows + 1, 0:128] = losses
    send[rows:, :] = jnp.zeros((8, 2 * step), jnp.float32)
    send[rows : rows + 1, 0:128] = losses


def pair_terms(numbers, masks, ids_here, unit_bf, blocks, cuts, old=None, final=None, window=None):
    window = window or (0, unit_bf.shape[0])
    rows, width = window[1] - window[0], unit_bf.shape[1]
    total = sum(count for _, _, count, _ in cuts)
    args = [numbers, *masks, ids_here, unit_bf, *blocks]
    scratch = [pltpu.VMEM((total, width), jnp.bfloat16)]
    if old is not None:
        args += old
    if final is not None:
        args += final
        shapes = [jax.ShapeDtypeStruct((rows + 8, width // 2), jnp.float32)] * 2
        scratch += [pltpu.VMEM((rows, width), jnp.float32)]
    else:
        shapes = [
            jax.ShapeDtypeStruct((rows, width), jnp.float32),
            jax.ShapeDtypeStruct((8, 128), jnp.float32),
        ]
    return pl.pallas_call(
        functools.partial(pair_kernel, cuts, old is None, final is not None, window),
        out_shape=shapes,
        in_specs=[VMEM] * len(args),
        out_specs=[VMEM] * len(shapes),
        scratch_shapes=scratch,
        compiler_params=pltpu.CompilerParams(vmem_limit_bytes=28 << 20),
        cost_estimate=pl.CostEstimate(flops=4 * rows * width * total, bytes_accessed=8 * rows * width, transcendentals=3 * rows * total),
        name="pair_terms",
    )(*args)


def combine_kernel(keep, arrived, own, send):
    rows, step = own.shape[0] - 8, own.shape[1]
    own[...] = keep[:, :step] + arrived[:, :step]
    for k in range(step // LANES):
        at = slice(step + k * LANES, step + (k + 1) * LANES)
        value = keep[:rows, at] + arrived[:rows, at]
        send[k * rows : (k + 1) * rows] = value.astype(jnp.bfloat16)
    losses = keep[rows : rows + 1, 0:128] + arrived[rows : rows + 1, 0:128]
    high = losses.astype(jnp.bfloat16).astype(jnp.float32)
    middle = (losses - high).astype(jnp.bfloat16).astype(jnp.float32)
    low = losses - high - middle
    line = lax.broadcasted_iota(jnp.int32, (FACTS, LANES), 0)
    packed = jnp.where(line == 0, high, jnp.where(line == 1, middle, jnp.where(line == 2, low, 0.0)))
    send[step // LANES * rows :] = packed.astype(jnp.bfloat16)


def combine(keep, arrived):
    rows, width = keep.shape[0] - 8, keep.shape[1]
    return pl.pallas_call(
        combine_kernel,
        out_shape=[
            jax.ShapeDtypeStruct((rows + 8, width // 2), jnp.float32),
            jax.ShapeDtypeStruct((rows * (width // 2 // LANES) + FACTS, LANES), jnp.bfloat16),
        ],
        in_specs=[VMEM] * 2,
        out_specs=[VMEM] * 2,
        compiler_params=pltpu.CompilerParams(vmem_limit_bytes=16 << 20),
        cost_estimate=pl.CostEstimate(flops=rows * width, bytes_accessed=8 * rows * width, transcendentals=0),
        name="combine",
    )(keep, arrived)


def gradient_kernel(own_a, own_b, arrived_a, arrived_b, features, grad, loss, draw, parts, value, sems):
    rows = features.shape[1]
    half = rows // 2
    steps, height = parts.shape[:2]
    total = own_a[half : half + 1, 0:128] + own_b[half : half + 1, 0:128]
    for arrived in (arrived_a, arrived_b):
        low = arrived[arrived.shape[0] - FACTS :].astype(jnp.float32)
        total += jnp.sum(low, axis=0, keepdims=True)
    lane = lax.broadcasted_iota(jnp.int32, (1, 128), 1)
    mine = jnp.where(lane == lax.axis_index("group"), total, 0.0)
    value[...] = jnp.sum(mine, axis=1, keepdims=True) / (rows * rows)
    copies = [pltpu.make_async_copy(value, loss, sems.at[steps])]
    copies[0].start()
    for begin, own, arrived in ((0, own_a, arrived_a), (half, own_b, arrived_b)):
        for k in range(draw.shape[1] // LANES):
            at = slice(k * LANES, (k + 1) * LANES)
            value = own[:half, at] + arrived[k * half : (k + 1) * half].astype(jnp.float32)
            draw[begin : begin + half, at] = value.astype(jnp.bfloat16)
    for k in range(steps):
        at = pl.ds(k * height, height)
        parts[k] = jnp.dot(features[at], draw[...], preferred_element_type=jnp.float32)
        copies.append(pltpu.make_async_copy(parts.at[k], grad.at[at], sems.at[k]))
        copies[-1].start()
    for copy in copies:
        copy.wait()


def gradient(own, arrived, features_t):
    depth, rows = features_t.shape
    width = own[0].shape[1]
    steps = 6
    return pl.pallas_call(
        gradient_kernel,
        out_shape=[
            jax.ShapeDtypeStruct((depth, width), jnp.float32),
            jax.ShapeDtypeStruct((1, 1), jnp.float32),
        ],
        in_specs=[VMEM] * 5,
        out_specs=[ANY, ANY],
        scratch_shapes=[
            pltpu.VMEM((rows, width), jnp.bfloat16),
            pltpu.VMEM((steps, depth // steps, width), jnp.float32),
            pltpu.VMEM((1, 1), jnp.float32),
            pltpu.SemaphoreType.DMA((steps + 1,)),
        ],
        compiler_params=pltpu.CompilerParams(vmem_limit_bytes=16 << 20),
        cost_estimate=pl.CostEstimate(
            flops=2 * rows * depth * width, bytes_accessed=4 * depth * width, transcendentals=0
        ),
        name="gradient",
    )(*own, *arrived, features_t)


def small_plan(features, matrix, ids, filled, mask, scale, shift):
    rows = features.shape[0]
    part = rows // 4

    mine = part_unit(ids, filled, features, matrix)
    mask = jnp.broadcast_to(after(mask, mine)[:, None], (8, 128))
    far = trade(mine, 6, 0)
    near = trade(mine, 1, 0)
    side = trade(mine, 2, 0)
    unit, unit_bf, length, column, numbers = whole_unit(
        ids, filled, scale, shift, after(features, mine), matrix
    )
    others = [swap(mask, "group", k) for k in (1, 2, 3)]
    far_s = trade(after(far, unit_bf, *others), 2, 0)
    far_x = trade(after(far, unit_bf, *others), 1, 0)
    side_x = trade(after(side, unit_bf, near), 1, 0)
    common = (numbers, [mask, *others], column, unit_bf)
    early = pair_terms(
        *common, [near, side, far], ((1, 0, part, 0), (2, 0, part, 1), (6, 0, part, 2))
    )
    last = trade(after(far_x, early[1]), 2, 0)
    middle = pair_terms(
        *common, [far_s, far_x], ((4, 0, part, 0), (7, 0, part, 1)), old=early
    )
    middle = pair_terms(*common, [side_x], ((3, 0, part, 0),), old=middle)
    own, arrived = [], []
    sent = []
    for window in ((0, rows // 2), (rows // 2, rows)):
        keep, send = pair_terms(
            *common,
            [last],
            ((5, 0, part, 0),),
            old=middle,
            final=[unit, length],
            window=window,
        )
        sent.append((keep, swap(send, "group", 1)))
    for keep, received in sent:
        kept, send = combine(keep, received)
        own.append(kept)
        arrived.append(swap(send, "group", 2))
    return gradient(own, arrived, features.T)


def scatter_sum(block):
    count = lax.axis_size("group")
    me = lax.axis_index("group")
    rows, columns = block.shape
    block = block.reshape(rows, count, columns // count)
    kept = count
    for bit in range(count.bit_length() - 1):
        mine = jnp.bitwise_and(jnp.right_shift(me, bit), 1)
        pairs = block.reshape(rows, kept // 2, 2, -1)
        keep = lax.dynamic_index_in_dim(pairs, mine, 2, keepdims=False)
        send = lax.dynamic_index_in_dim(pairs, 1 - mine, 2, keepdims=False)
        if bit > 0:
            send = send.astype(jnp.bfloat16)
        block = keep + swap(send, "group", 1 << bit).astype(jnp.float32)
        kept //= 2
    return block.reshape(rows, columns // count)


def large_plan(features, matrix, ids, filled, mask, scale, shift):
    rows = features.shape[0]
    unit, length = project(features, matrix)
    unit_bf = unit.astype(jnp.bfloat16)
    current = (unit_bf, ids, filled)
    for bit in range(lax.axis_size("peer").bit_length() - 1):
        arrived = [swap(value, "peer", 1 << bit) for value in current]
        chosen = jnp.bitwise_and(jnp.right_shift(mask[0], bit), 1) == 1
        current = [jnp.where(chosen, new, old) for new, old in zip(arrived, current)]
    theirs, their_ids, their_filled = current
    scores = lax.dot_general(
        unit_bf, theirs, (((1,), (1,)), ((), ())), preferred_element_type=jnp.float32
    )
    index = jnp.arange(rows, dtype=jnp.int32)
    used = (index < filled[0])[:, None] & (index < their_filled[0])[None]
    signs = jnp.where(ids[:, None] == their_ids[None], 1.0, -1.0).astype(jnp.float32)
    logits = scale[0] * scores + shift[0]
    loss = jnp.sum(jnp.where(used, jax.nn.softplus(-signs * logits), 0.0))
    slopes = jnp.where(used, -signs * jax.nn.sigmoid(-signs * logits) * scale[0], 0.0)
    dunit = jnp.dot(slopes.astype(jnp.bfloat16), theirs, preferred_element_type=jnp.float32)
    tangent = (dunit - unit * jnp.sum(unit * dunit, axis=1, keepdims=True)) / length
    draw = scatter_sum(tangent).astype(jnp.bfloat16)
    grad = lax.dot_general(
        features, draw, (((0,), (0,)), ((), ())), preferred_element_type=jnp.float32
    )
    return (grad, (loss / (rows * rows)).reshape(1, 1))


def on_device(
    view_descriptors,
    embedding_matrix,
    picture_of_view,
    filled_view_places,
    companion_masks,
    score_scale,
    score_shift,
):
    small = lax.axis_size("peer") == 8 and lax.axis_size("group") == 4
    plan = small_plan if small else large_plan
    return plan(
        view_descriptors,
        embedding_matrix,
        picture_of_view,
        filled_view_places,
        companion_masks,
        score_scale,
        score_shift,
    )


def solution(mesh):
    placed = (P("peer", None), P(), P("peer"), P("peer"), P("group"), P(), P())
    return jax.shard_map(
        on_device,
        mesh=mesh,
        in_specs=placed,
        out_specs=(P("peer", "group"), P("peer", "group")),
        check_vma=False,
    )
```

```python
import functools

import jax
import jax.numpy as jnp
from jax import lax
from jax.experimental import pallas as pl
from jax.experimental.pallas import tpu as pltpu
from jax.sharding import PartitionSpec as P

AXES = ("peer", "group")
STEPS = 3
FACTS = 16
LANES = 128
SMALL = pl.CostEstimate(flops=1, bytes_accessed=1, transcendentals=0)
ANY = pl.BlockSpec(memory_space=pl.ANY)
VMEM = pl.BlockSpec(memory_space=pltpu.VMEM)


def swap(block, axis, mask):
    count = lax.axis_size(axis)
    return lax.ppermute(block, axis, [(i, i ^ mask) for i in range(count)])


def trade(block, peer_mask, member_mask):
    members = lax.axis_size("group")
    route = []
    for p in range(lax.axis_size("peer")):
        for g in range(members):
            other = (p ^ peer_mask) * members + (g ^ member_mask)
            route.append((p * members + g, other))
    return lax.ppermute(block, AXES, route)


def project(view_descriptors, embedding_matrix):
    raw = jnp.dot(view_descriptors, embedding_matrix, preferred_element_type=jnp.float32)
    row_length = jnp.sqrt(jnp.sum(raw * raw, axis=1, keepdims=True) + 1e-06)
    return (raw / row_length, row_length)


def after(value, *others):
    return lax.optimization_barrier((value, *others))[0]


def load(features, matrix, features_v, matrix_v, sems, begin, rows):
    depth = matrix_v.shape[0] // STEPS
    copies = [pltpu.make_async_copy(features.at[pl.ds(begin, rows)], features_v, sems.at[STEPS])]
    for k in range(STEPS):
        at = pl.ds(k * depth, depth)
        copies.append(pltpu.make_async_copy(matrix.at[at], matrix_v.at[at], sems.at[k]))
    for copy in copies:
        copy.start()
    return copies


def multiply(copies, features_v, matrix_v, raw):
    depth = matrix_v.shape[0] // STEPS
    copies[0].wait()
    for k in range(STEPS):
        at = slice(k * depth, (k + 1) * depth)
        copies[1 + k].wait()
        part = jnp.dot(features_v[:, at], matrix_v[at], preferred_element_type=jnp.float32)
        raw[...] = part if k == 0 else raw[...] + part
    return jnp.sqrt(jnp.sum(raw[...] * raw[...], axis=1, keepdims=True) + 1e-06)


def part_unit_kernel(ids, filled, features, matrix, unit, ids_v, filled_s, features_v, matrix_v, raw, sems, small_sems):
    rows, width = raw.shape
    me = lax.axis_index("group")
    small = [
        pltpu.make_async_copy(ids, ids_v, small_sems.at[0]),
        pltpu.make_async_copy(filled, filled_s, small_sems.at[1]),
    ]
    for copy in small:
        copy.start()
    copies = load(features, matrix, features_v, matrix_v, sems, me * rows, rows)
    for copy in small:
        copy.wait()
    all_ids = ids_v[...].reshape(1, 4 * rows)
    here = all_ids[:, :rows]
    for k in range(1, 4):
        here = jnp.where(me == k, all_ids[:, k * rows : (k + 1) * rows], here)
    here = jnp.concatenate([here, jnp.zeros((1, LANES - rows), jnp.int32)], axis=1)
    count = jnp.full((1, LANES), filled_s[0], jnp.int32)
    row = lax.broadcasted_iota(jnp.int32, (FACTS, LANES), 0)
    facts = jnp.zeros((FACTS, LANES), jnp.int32)
    for k, digit in enumerate((here & 255, here >> 8, count & 255, count >> 8)):
        facts = jnp.where(row == k, digit, facts)
    inverse = 1.0 / multiply(copies, features_v, matrix_v, raw)
    chunks = width // LANES
    for k in range(chunks):
        value = raw[:, k * LANES : (k + 1) * LANES] * inverse
        unit[k * rows : (k + 1) * rows] = value.astype(jnp.bfloat16)
    unit[chunks * rows :] = facts.astype(jnp.float32).astype(jnp.bfloat16)


def part_unit(ids, filled, features, matrix):
    rows, depth = features.shape
    width = matrix.shape[1]
    part = rows // 4
    return pl.pallas_call(
        part_unit_kernel,
        out_shape=jax.ShapeDtypeStruct((part * width // LANES + FACTS, LANES), jnp.bfloat16),
        in_specs=[ANY] * 4,
        out_specs=VMEM,
        scratch_shapes=[
            pltpu.VMEM((rows,), jnp.int32),
            pltpu.SMEM((1,), jnp.int32),
            pltpu.VMEM((part, depth), jnp.bfloat16),
            pltpu.VMEM((depth, width), jnp.bfloat16),
            pltpu.VMEM((part, width), jnp.float32),
            pltpu.SemaphoreType.DMA((STEPS + 1,)),
            pltpu.SemaphoreType.DMA((2,)),
        ],
        compiler_params=pltpu.CompilerParams(vmem_limit_bytes=60 << 20),
        cost_estimate=pl.CostEstimate(
            flops=rows * depth * width, bytes_accessed=2 * depth * width, transcendentals=0
        ),
        name="part_unit",
    )(ids, filled, features, matrix)


def whole_unit_kernel(ids, filled, scale, shift, features, matrix, unit, unit_bf, inverse, column, numbers, features_v, matrix_v, sems):
    rows = unit.shape[0]
    copies = load(features, matrix, features_v, matrix_v, sems, 0, rows)
    column[...] = jnp.broadcast_to(ids[...].reshape(1, rows).astype(jnp.float32), (128, rows)).T
    numbers[0:1] = jnp.broadcast_to(scale[...].reshape(1, 1), (1, 128))
    numbers[1:2] = jnp.broadcast_to(shift[...].reshape(1, 1), (1, 128))
    numbers[2:3] = jnp.broadcast_to(filled[...].reshape(1, 1), (1, 128)).astype(jnp.float32)
    numbers[3:] = jnp.zeros((5, 128), jnp.float32)
    factor = 1.0 / multiply(copies, features_v, matrix_v, unit)
    inverse[...] = jnp.broadcast_to(factor, inverse.shape)
    value = unit[...] * factor
    unit[...] = value
    unit_bf[...] = value.astype(jnp.bfloat16)


def whole_unit(ids, filled, scale, shift, features, matrix):
    rows, depth = features.shape
    width = matrix.shape[1]
    return pl.pallas_call(
        whole_unit_kernel,
        out_shape=[
            jax.ShapeDtypeStruct((rows, width), jnp.float32),
            jax.ShapeDtypeStruct((rows, width), jnp.bfloat16),
            jax.ShapeDtypeStruct((rows, 128), jnp.float32),
            jax.ShapeDtypeStruct((rows, 128), jnp.float32),
            jax.ShapeDtypeStruct((8, 128), jnp.float32),
        ],
        in_specs=[VMEM] * 4 + [ANY] * 2,
        out_specs=[VMEM] * 5,
        scratch_shapes=[
            pltpu.VMEM((rows, depth), jnp.bfloat16),
            pltpu.VMEM((depth, width), jnp.bfloat16),
            pltpu.SemaphoreType.DMA((STEPS + 1,)),
        ],
        compiler_params=pltpu.CompilerParams(vmem_limit_bytes=28 << 20),
        cost_estimate=pl.CostEstimate(
            flops=2 * rows * depth * width, bytes_accessed=4 * depth * width, transcendentals=0
        ),
        name="whole_unit",
    )(ids, filled, scale, shift, features, matrix)


def pair_kernel(cuts, first, final, window, *refs):
    refs = list(refs)
    numbers = refs[0]
    masks = [ref[0:1] for ref in refs[1:5]]
    ids_here, unit_bf = refs[5:7]
    del refs[:7]
    blocks = [refs.pop(0) for _ in cuts]
    if not first:
        old_dunit, old_losses = refs.pop(0), refs.pop(0)
    if final:
        unit, inverse = refs.pop(0), refs.pop(0)
        keep, send, stacked, total = refs
    else:
        total, losses_out, stacked = refs
    me = lax.axis_index("group")
    here = slice(*window)
    rows = window[1] - window[0]
    part = unit_bf.shape[0] // 4
    offset = 0
    for block, (_, _, count, _) in zip(blocks, cuts):
        for k in range(stacked.shape[1] // LANES):
            at = slice(k * LANES, (k + 1) * LANES)
            stacked[offset : offset + count, at] = block[k * count : (k + 1) * count]
        offset += count
    scores = lax.dot_general(
        unit_bf[here], stacked[...], (((1,), (1,)), ((), ())), preferred_element_type=jnp.float32
    )
    row = window[0] + lax.broadcasted_iota(jnp.int32, (rows, 1), 0)
    used_here = row < numbers[2:3, 0:1].astype(jnp.int32)
    lane = lax.broadcasted_iota(jnp.int32, (1, 128), 1)
    losses = jnp.zeros((1, 128), jnp.float32) if first or window[0] else old_losses[0:1]
    slopes = []
    offset = 0
    for mask, begin, count, owner in cuts:
        turn = jnp.full((1, 128), -1, jnp.int32)
        for e, other in enumerate(masks):
            turn = jnp.where(other == mask, jnp.bitwise_xor(me, e), turn)
        last = blocks[owner].shape[0] - FACTS
        fact = blocks[owner][last:].astype(jnp.float32)
        ids = fact[0:1, begin : begin + count] + 256.0 * fact[1:2, begin : begin + count]
        filled = fact[2:3, :count] + 256.0 * fact[3:4, :count]
        place = me * part + begin + lax.broadcasted_iota(jnp.int32, (1, count), 1)
        there = (place < filled.astype(jnp.int32)) & (turn[:, :count] >= 0)
        used = used_here & there
        signs = jnp.where(ids_here[here, :1] == ids, -1.0, 1.0)
        scale, shift = numbers[0:1, :count], numbers[1:2, :count]
        logits = signs * (scale * scores[:, offset : offset + count] + shift)
        small = jnp.exp(-jnp.abs(logits))
        penalty = jnp.maximum(logits, 0.0) + jnp.log1p(small)
        loss = jnp.sum(jnp.where(used, penalty, 0.0))
        losses = losses + jnp.where(lane == turn, loss, 0.0)
        gate = jnp.where(logits >= 0, 1.0, small) / (1.0 + small)
        slopes.append(jnp.where(used, signs * gate * scale, 0.0).astype(jnp.bfloat16))
        offset += count
    slopes = slopes[0] if len(slopes) == 1 else jnp.concatenate(slopes, axis=1)
    width = stacked.shape[1]
    step = width // 4
    for k in range(4):
        at = slice(k * step, (k + 1) * step)
        part = jnp.dot(slopes, stacked[:, at], preferred_element_type=jnp.float32)
        total[:, at] = part if first else old_dunit[here, at] + part
    if not final:
        losses_out[...] = jnp.broadcast_to(losses, losses_out.shape)
        return
    along = jnp.sum(unit[here] * total[...], axis=1, keepdims=True)
    for k, other in enumerate((0, 2)):
        for out, member in ((keep, other), (send, other + 1)):
            at = pl.ds(pl.multiple_of(jnp.bitwise_xor(me, member) * step, 128), step)
            value = (total[:, at] - unit[here, at] * along) * inverse[here, :1]
            out[:rows, k * step : (k + 1) * step] = value
    keep[rows:, :] = jnp.zeros((8, 2 * step), jnp.float32)
    keep[rows : rows + 1, 0:128] = losses
    send[rows:, :] = jnp.zeros((8, 2 * step), jnp.float32)
    send[rows : rows + 1, 0:128] = losses


def pair_terms(numbers, masks, ids_here, unit_bf, blocks, cuts, old=None, final=None, window=None):
    window = window or (0, unit_bf.shape[0])
    rows, width = window[1] - window[0], unit_bf.shape[1]
    total = sum(count for _, _, count, _ in cuts)
    args = [numbers, *masks, ids_here, unit_bf, *blocks]
    scratch = [pltpu.VMEM((total, width), jnp.bfloat16)]
    if old is not None:
        args += old
    if final is not None:
        args += final
        shapes = [jax.ShapeDtypeStruct((rows + 8, width // 2), jnp.float32)] * 2
        scratch += [pltpu.VMEM((rows, width), jnp.float32)]
    else:
        shapes = [
            jax.ShapeDtypeStruct((rows, width), jnp.float32),
            jax.ShapeDtypeStruct((8, 128), jnp.float32),
        ]
    return pl.pallas_call(
        functools.partial(pair_kernel, cuts, old is None, final is not None, window),
        out_shape=shapes,
        in_specs=[VMEM] * len(args),
        out_specs=[VMEM] * len(shapes),
        scratch_shapes=scratch,
        compiler_params=pltpu.CompilerParams(vmem_limit_bytes=28 << 20),
        cost_estimate=pl.CostEstimate(flops=4 * rows * width * total, bytes_accessed=8 * rows * width, transcendentals=3 * rows * total),
        name="pair_terms",
    )(*args)


def combine_kernel(keep, arrived, own, send):
    rows, step = own.shape[0] - 8, own.shape[1]
    own[...] = keep[:, :step] + arrived[:, :step]
    for k in range(step // LANES):
        at = slice(step + k * LANES, step + (k + 1) * LANES)
        value = keep[:rows, at] + arrived[:rows, at]
        send[k * rows : (k + 1) * rows] = value.astype(jnp.bfloat16)
    losses = keep[rows : rows + 1, 0:128] + arrived[rows : rows + 1, 0:128]
    high = losses.astype(jnp.bfloat16).astype(jnp.float32)
    middle = (losses - high).astype(jnp.bfloat16).astype(jnp.float32)
    low = losses - high - middle
    line = lax.broadcasted_iota(jnp.int32, (FACTS, LANES), 0)
    packed = jnp.where(line == 0, high, jnp.where(line == 1, middle, jnp.where(line == 2, low, 0.0)))
    send[step // LANES * rows :] = packed.astype(jnp.bfloat16)


def combine(keep, arrived):
    rows, width = keep.shape[0] - 8, keep.shape[1]
    return pl.pallas_call(
        combine_kernel,
        out_shape=[
            jax.ShapeDtypeStruct((rows + 8, width // 2), jnp.float32),
            jax.ShapeDtypeStruct((rows * (width // 2 // LANES) + FACTS, LANES), jnp.bfloat16),
        ],
        in_specs=[VMEM] * 2,
        out_specs=[VMEM] * 2,
        compiler_params=pltpu.CompilerParams(vmem_limit_bytes=16 << 20),
        cost_estimate=pl.CostEstimate(flops=rows * width, bytes_accessed=8 * rows * width, transcendentals=0),
        name="combine",
    )(keep, arrived)


def gradient_kernel(own_a, own_b, arrived_a, arrived_b, features, grad, loss, draw, parts, value, sems):
    rows = features.shape[1]
    half = rows // 2
    steps, height = parts.shape[:2]
    total = own_a[half : half + 1, 0:128] + own_b[half : half + 1, 0:128]
    for arrived in (arrived_a, arrived_b):
        low = arrived[arrived.shape[0] - FACTS :].astype(jnp.float32)
        total += jnp.sum(low, axis=0, keepdims=True)
    lane = lax.broadcasted_iota(jnp.int32, (1, 128), 1)
    mine = jnp.where(lane == lax.axis_index("group"), total, 0.0)
    value[...] = jnp.sum(mine, axis=1, keepdims=True) / (rows * rows)
    copies = [pltpu.make_async_copy(value, loss, sems.at[steps])]
    copies[0].start()
    for begin, own, arrived in ((0, own_a, arrived_a), (half, own_b, arrived_b)):
        for k in range(draw.shape[1] // LANES):
            at = slice(k * LANES, (k + 1) * LANES)
            value = own[:half, at] + arrived[k * half : (k + 1) * half].astype(jnp.float32)
            draw[begin : begin + half, at] = value.astype(jnp.bfloat16)
    for k in range(steps):
        at = pl.ds(k * height, height)
        parts[k] = jnp.dot(features[at], draw[...], preferred_element_type=jnp.float32)
        copies.append(pltpu.make_async_copy(parts.at[k], grad.at[at], sems.at[k]))
        copies[-1].start()
    for copy in copies:
        copy.wait()


def gradient(own, arrived, features_t):
    depth, rows = features_t.shape
    width = own[0].shape[1]
    steps = 6
    return pl.pallas_call(
        gradient_kernel,
        out_shape=[
            jax.ShapeDtypeStruct((depth, width), jnp.float32),
            jax.ShapeDtypeStruct((1, 1), jnp.float32),
        ],
        in_specs=[VMEM] * 5,
        out_specs=[ANY, ANY],
        scratch_shapes=[
            pltpu.VMEM((rows, width), jnp.bfloat16),
            pltpu.VMEM((steps, depth // steps, width), jnp.float32),
            pltpu.VMEM((1, 1), jnp.float32),
            pltpu.SemaphoreType.DMA((steps + 1,)),
        ],
        compiler_params=pltpu.CompilerParams(vmem_limit_bytes=16 << 20),
        cost_estimate=pl.CostEstimate(
            flops=2 * rows * depth * width, bytes_accessed=4 * depth * width, transcendentals=0
        ),
        name="gradient",
    )(*own, *arrived, features_t)


def small_plan(features, matrix, ids, filled, mask, scale, shift):
    rows = features.shape[0]
    part = rows // 4

    mine = part_unit(ids, filled, features, matrix)
    mask = jnp.broadcast_to(after(mask, mine)[:, None], (8, 128))
    far = trade(mine, 6, 0)
    near = trade(mine, 1, 0)
    side = trade(mine, 2, 0)
    unit, unit_bf, inverse, column, numbers = whole_unit(
        ids, filled, scale, shift, after(features, mine), matrix
    )
    others = [swap(mask, "group", k) for k in (1, 2, 3)]
    far_s = trade(after(far, unit_bf, *others), 2, 0)
    far_x = trade(after(far, unit_bf, *others), 1, 0)
    side_x = trade(after(side, unit_bf, near), 1, 0)
    common = (numbers, [mask, *others], column, unit_bf)
    early = pair_terms(
        *common, [near, side, far], ((1, 0, part, 0), (2, 0, part, 1), (6, 0, part, 2))
    )
    last = trade(after(far_x, early[1]), 2, 0)
    middle = pair_terms(
        *common, [far_s, far_x], ((4, 0, part, 0), (7, 0, part, 1)), old=early
    )
    middle = pair_terms(*common, [side_x], ((3, 0, part, 0),), old=middle)
    own, arrived = [], []
    sent = []
    for window in ((0, rows // 2), (rows // 2, rows)):
        keep, send = pair_terms(
            *common,
            [last],
            ((5, 0, part, 0),),
            old=middle,
            final=[unit, inverse],
            window=window,
        )
        sent.append((keep, swap(send, "group", 1)))
    for keep, received in sent:
        kept, send = combine(keep, received)
        own.append(kept)
        arrived.append(swap(send, "group", 2))
    return gradient(own, arrived, features.T)


def scatter_sum(block):
    count = lax.axis_size("group")
    me = lax.axis_index("group")
    rows, columns = block.shape
    block = block.reshape(rows, count, columns // count)
    kept = count
    for bit in range(count.bit_length() - 1):
        mine = jnp.bitwise_and(jnp.right_shift(me, bit), 1)
        pairs = block.reshape(rows, kept // 2, 2, -1)
        keep = lax.dynamic_index_in_dim(pairs, mine, 2, keepdims=False)
        send = lax.dynamic_index_in_dim(pairs, 1 - mine, 2, keepdims=False)
        if bit > 0:
            send = send.astype(jnp.bfloat16)
        block = keep + swap(send, "group", 1 << bit).astype(jnp.float32)
        kept //= 2
    return block.reshape(rows, columns // count)


def large_plan(features, matrix, ids, filled, mask, scale, shift):
    rows = features.shape[0]
    unit, length = project(features, matrix)
    unit_bf = unit.astype(jnp.bfloat16)
    current = (unit_bf, ids, filled)
    for bit in range(lax.axis_size("peer").bit_length() - 1):
        arrived = [swap(value, "peer", 1 << bit) for value in current]
        chosen = jnp.bitwise_and(jnp.right_shift(mask[0], bit), 1) == 1
        current = [jnp.where(chosen, new, old) for new, old in zip(arrived, current)]
    theirs, their_ids, their_filled = current
    scores = lax.dot_general(
        unit_bf, theirs, (((1,), (1,)), ((), ())), preferred_element_type=jnp.float32
    )
    index = jnp.arange(rows, dtype=jnp.int32)
    used = (index < filled[0])[:, None] & (index < their_filled[0])[None]
    signs = jnp.where(ids[:, None] == their_ids[None], 1.0, -1.0).astype(jnp.float32)
    logits = scale[0] * scores + shift[0]
    loss = jnp.sum(jnp.where(used, jax.nn.softplus(-signs * logits), 0.0))
    slopes = jnp.where(used, -signs * jax.nn.sigmoid(-signs * logits) * scale[0], 0.0)
    dunit = jnp.dot(slopes.astype(jnp.bfloat16), theirs, preferred_element_type=jnp.float32)
    tangent = (dunit - unit * jnp.sum(unit * dunit, axis=1, keepdims=True)) / length
    draw = scatter_sum(tangent).astype(jnp.bfloat16)
    grad = lax.dot_general(
        features, draw, (((0,), (0,)), ((), ())), preferred_element_type=jnp.float32
    )
    return (grad, (loss / (rows * rows)).reshape(1, 1))


def on_device(
    view_descriptors,
    embedding_matrix,
    picture_of_view,
    filled_view_places,
    companion_masks,
    score_scale,
    score_shift,
):
    small = lax.axis_size("peer") == 8 and lax.axis_size("group") == 4
    plan = small_plan if small else large_plan
    return plan(
        view_descriptors,
        embedding_matrix,
        picture_of_view,
        filled_view_places,
        companion_masks,
        score_scale,
        score_shift,
    )


def solution(mesh):
    placed = (P("peer", None), P(), P("peer"), P("peer"), P("group"), P(), P())
    return jax.shard_map(
        on_device,
        mesh=mesh,
        in_specs=placed,
        out_specs=(P("peer", "group"), P("peer", "group")),
        check_vma=False,
    )
```
